128 devices in a mesh: ctx: 16 (over x, z), tp: 8 (over y, core).
Axes of the slice: x: 4, y: 4, z: 4, core: 2. Of those that a mesh axis runs over, the one named last changes fastest.
Arguments:
- tokens: bfloat16 [8192, 4096], P('ctx', 'tp'), may hold values from -6 to 6
- w_query: bfloat16 [4096, 2048], P(None, 'tp'), may hold values from -0.09375 to 0.09375
- w_key: bfloat16 [4096, 2048], P(None, 'tp'), may hold values from -0.09375 to 0.09375
- w_value: bfloat16 [4096, 4096], P(None, 'tp'), may hold values from -0.09375 to 0.09375
- w_gate: bfloat16 [4096, 4096], P(None, 'tp'), may hold values from -0.09375 to 0.09375
- w_out: bfloat16 [4096, 4096], P('tp'), may hold values from -0.125 to 0.125
- log_decay: float32 [8, 8192], P('tp', 'ctx'), may hold values from -0.7 to 0
Outputs:
- mixed: bfloat16 [8192, 4096], P('ctx', 'tp')
The draws below stay inside these ranges and needn't reach their ends.
All inputs are finite; a program needn't handle non-finite values.
Results may differ from the reference program's by a relative error of at most 0.023.
Values may be sent and summed in bfloat16 or wider, within the bound.
No kernel may reach another device: no remote copies, remote signals or barrier semaphores. Data moves between devices by JAX's collectives and lax.ppermute only.
A program may use at most 128 MiB of HBM per device.

```python
import math
import jax
import jax.numpy as jnp
from jax import lax

D = 4096
DK = 256
DV = 512
HEAD_GROUP = 8
TOK_DEV = 512
TOKEN_LENGTH = 8192


def draw_log_decay(key, part):
    key = jax.random.fold_in(key, 7)
    key_collection = jax.random.split(key, 6)
    order = jax.random.permutation(key_collection[0], HEAD_GROUP)
    fast_count = HEAD_GROUP // 2
    fast_heads = order < fast_count
    random_offset = jnp.exp(jax.random.uniform(key_collection[1], (HEAD_GROUP, TOKEN_LENGTH), jnp.float32, -math.log(2.0), math.log(2.0)))
    fast_rate = 1.0 / jax.random.uniform(key_collection[2], (HEAD_GROUP,), jnp.float32, 30.0, 50.0)
    slow_rate = jax.random.uniform(key_collection[3], (HEAD_GROUP,), jnp.float32, 0.1, 0.6) / TOKEN_LENGTH
    baseline_decay = jnp.where(fast_heads, fast_rate, slow_rate)
    spike_positions = jax.random.randint(key_collection[4], (2, HEAD_GROUP), 0, TOKEN_LENGTH)
    token_index = jnp.arange(TOKEN_LENGTH)[None, :]
    spike_flag = (token_index == spike_positions[0][:, None]) | (token_index == spike_positions[1][:, None])
    spike_decay_drop = jax.random.uniform(key_collection[5], (HEAD_GROUP, TOKEN_LENGTH), jnp.float32, math.log(0.5), math.log(0.8))
    return jnp.where(spike_flag, spike_decay_drop, -baseline_decay[:, None] * random_offset).astype(jnp.float32)


def with_spikes(drawn, own_key, source, target, blocks, factor):
    def block_of(position):
        return (jnp.arange(drawn.shape[position]) // (drawn.shape[position] // blocks)).reshape((-1,) + (1,) * (drawn.ndim - 1 - position))

    one_side = jax.random.permutation(own_key, blocks)[block_of(target)]
    other_side = (block_of(target) + blocks // 2) % blocks
    return jnp.where((block_of(source) == one_side) | (block_of(source) == other_side), factor * drawn, drawn)


def block_scale(stream_key, extent, cuts, smallest, top_value):
    gain = 1.0
    for position, blocks in cuts:
        draws = jax.random.uniform(jax.random.fold_in(jax.random.fold_in(stream_key, 6), position), (blocks,), jnp.float32, smallest / len(cuts), top_value / len(cuts))
        gain = gain * jnp.repeat(jnp.exp(draws), extent[position] // blocks).reshape((-1,) + (1,) * (len(extent) - 1 - position))
    return gain


def scatter_about(stream_key, shape, deviation, most, shards=(), dtype=jnp.bfloat16):
    level = block_scale(stream_key, shape, shards, -0.22, 0.18) if shards else 1.0
    result = jax.random.normal(stream_key, shape, jnp.float32) * deviation * level
    return jnp.minimum(jnp.maximum(result, -most), most).astype(dtype)


def noise_with(key, extent, scale, bound, shards, heavy, kind=jnp.bfloat16):
    values = scale * jax.random.normal(key, extent, jnp.float32)
    if shards:
        values = values * block_scale(key, extent, shards, -0.22, 0.18)
    return jnp.clip(with_spikes(values, jax.random.fold_in(key, 3), *heavy), -bound, bound).astype(kind)


def setup_inputs(seed: int = 0) -> dict:
    streams_of = jax.random.split(jax.random.key(seed), 8)
    tokens = scatter_about(streams_of[0], (TOKEN_LENGTH, D), 1.0, 6.0, ((0, 16), (1, 8)))
    w_query = scatter_about(streams_of[1], (D, HEAD_GROUP * DK), D ** -0.5, 0.09375, ((1, 8),))
    w_key = scatter_about(streams_of[2], (D, HEAD_GROUP * DK), D ** -0.5, 0.09375, ((1, 8),))
    w_value = scatter_about(streams_of[3], (D, HEAD_GROUP * DV), D ** -0.5, 0.09375, ((1, 8),))
    w_gate = scatter_about(streams_of[4], (D, HEAD_GROUP * DV), D ** -0.5, 0.09375, ((1, 8),))
    w_out = noise_with(streams_of[5], (HEAD_GROUP * DV, D), (HEAD_GROUP * DV) ** -0.5, 0.125, ((0, 8),), (0, 1, 8, 2.0))
    log_decay = draw_log_decay(jax.random.fold_in(streams_of[7], 71), 0)
    return {"tokens": tokens, "w_query": w_query, "w_key": w_key, "w_value": w_value, "w_gate": w_gate, "w_out": w_out, "log_decay": log_decay}


def block_terms(query_block, key_block, value_block, rate_block, state):
    length = query_block.shape[0]
    cumulative = jnp.cumsum(rate_block)
    spread = cumulative[:, None] - cumulative[None, :]
    lower_mask = jnp.arange(length)[:, None] >= jnp.arange(length)[None, :]
    weights = jnp.exp(jnp.where(lower_mask, spread, -1e+30))
    scores = jnp.dot(query_block, key_block.T, preferred_element_type=jnp.float32) * weights
    scores = scores.astype(jnp.bfloat16)
    inner_part = jnp.dot(scores, value_block, preferred_element_type=jnp.float32)
    carried = jnp.exp(cumulative)[:, None] * jnp.dot(query_block.astype(jnp.float32), state, precision=lax.Precision.HIGHEST)
    remain = jnp.exp(cumulative[-1] - cumulative)
    weighted_keys = key_block.astype(jnp.float32) * remain[:, None]
    new_state = jnp.exp(cumulative[-1]) * state + jnp.dot(weighted_keys.T, value_block.astype(jnp.float32), precision=lax.Precision.HIGHEST)
    return (inner_part + carried, new_state)

def group_norm(output):
    center = output - lax.optimization_barrier(jnp.mean(output, axis=-1, keepdims=True))
    variance = lax.optimization_barrier(jnp.mean(center * center, axis=-1, keepdims=True))
    return center * lax.rsqrt(variance + 1e-05)

def reference(tokens, w_query, w_key, w_value, w_gate, w_out, log_decay):
    queries = jnp.dot(tokens, w_query, preferred_element_type=jnp.float32).astype(jnp.bfloat16)
    keys = (jnp.dot(tokens, w_key, preferred_element_type=jnp.float32) * DK ** (-0.5)).astype(jnp.bfloat16)
    values = jnp.dot(tokens, w_value, preferred_element_type=jnp.float32).astype(jnp.bfloat16)
    gates = jnp.dot(tokens, w_gate, preferred_element_type=jnp.float32).astype(jnp.bfloat16)
    block_size = min(512, TOK_DEV)
    block_count = TOKEN_LENGTH // block_size
    pieces = []
    for head_index in range(HEAD_GROUP):
        query_head = queries[:, head_index * DK:(head_index + 1) * DK].reshape(block_count, block_size, DK)
        key_head = keys[:, head_index * DK:(head_index + 1) * DK].reshape(block_count, block_size, DK)
        value_head = values[:, head_index * DV:(head_index + 1) * DV].reshape(block_count, block_size, DV)
        rate_head = log_decay[head_index].reshape(block_count, block_size)

        def advance(state, inputs):
            output, new_state = block_terms(inputs[0], inputs[1], inputs[2], inputs[3], state)
            return (new_state, output)
        final_state, outputs = lax.scan(advance, jnp.zeros((DK, DV), jnp.float32), (query_head, key_head, value_head, rate_head))
        normed = group_norm(outputs.reshape(TOKEN_LENGTH, DV))
        gate_head = gates[:, head_index * DV:(head_index + 1) * DV].astype(jnp.float32)
        pieces.append(jax.nn.silu(gate_head) * normed)
    hidden = jnp.concatenate(pieces, axis=1).astype(jnp.bfloat16)
    return jnp.dot(hidden, w_out, preferred_element_type=jnp.float32).astype(jnp.bfloat16)
```

```python
import jax
import jax.numpy as jnp
from jax import lax
from jax.sharding import PartitionSpec as P

DK = 256
DV = 512
BF, F32 = jnp.bfloat16, jnp.float32
SIDE = 4


def tp_shift(value, step):
    pairs = [(i, (i + 2 * step) % 8) for i in range(8)]
    return lax.ppermute(value, "tp", pairs)


def tp_swap(value):
    return lax.ppermute(value, "tp", [(i, i ^ 1) for i in range(8)])


def z_flip(value, k):
    return lax.ppermute(value, "ctx", [(i, i ^ k) for i in range(16)])


def x_flip(value, k):
    return lax.ppermute(value, "ctx", [(i, i ^ (4 * k)) for i in range(16)])


def dot(a, b):
    return jnp.dot(a, b, preferred_element_type=F32)


def packed(piece, factor):
    high = lax.reduce_precision(factor, 8, 7)
    rows = jnp.concatenate([jnp.full((8, DV), high, F32), jnp.full((8, DV), factor - high, F32)])
    return jnp.concatenate([piece.astype(BF), rows.astype(BF)])


def unpacked(message):
    factor = message[64, 0].astype(F32) + message[72, 0].astype(F32)
    return message[:64].astype(F32), factor


def between(factors, sources, low, high):
    product = jnp.float32(1.0)
    for factor, source in zip(factors, sources):
        product = product * jnp.where((source > low) & (source < high), factor, 1.0)
    return product


def prefix(pieces, factors, sources, target):
    total = jnp.zeros_like(pieces[0])
    for piece, source in zip(pieces, sources):
        weight = jnp.where(source < target, between(factors, sources, source, target), 0.0)
        total = total + weight * piece
    return total


def shards(tokens, w_query, w_key, w_value, w_gate, w_out, log_decay):
    ctx, tp = lax.axis_index("ctx"), lax.axis_index("tp")
    x, z, y, core = ctx // SIDE, ctx % SIDE, tp // 2, tp % 2

    top, low = tokens[:256], tokens[256:]
    a_right, a_left = tp_shift(top, 1), tp_shift(low, -1)
    b_right, b_left = tp_shift(low, 1), tp_shift(top, -1)
    c_right, c_left = tp_shift(a_right, 1), tp_shift(a_left, -1)
    before = jnp.concatenate([a_right, b_right])
    after = jnp.concatenate([b_left, a_left])
    across = jnp.concatenate([c_right, c_left])
    parts = []
    for block, step in ((tokens, 0), (before, -1), (after, 1), (across, 2)):
        owner = (y + step) % SIDE
        parts.append((block, 2 * owner + core))
        parts.append((tp_swap(block), 2 * owner + 1 - core))

    w_out_blocks = w_out.reshape(DV, SIDE, 2, DV)
    w_own = lax.dynamic_index_in_dim(w_out_blocks, core, 2, keepdims=False)
    w_other = tp_swap(lax.dynamic_index_in_dim(w_out_blocks, 1 - core, 2, keepdims=False))

    def project(weight):
        total = 0.0
        for block, owner in parts:
            total = total + dot(block, lax.dynamic_slice_in_dim(weight, owner * 512, 512))
        return total

    keys = (project(w_key) * DK ** (-0.5)).astype(BF)
    values = project(w_value).astype(BF)
    cumul = jnp.cumsum(log_decay[0])
    remain = jnp.exp(cumul[-1] - cumul)
    factor = jnp.exp(cumul[-1])
    weighted = (keys.astype(F32) * remain[:, None]).astype(BF)
    state = lax.dot_general(weighted, values, (((0,), (0,)), ((), ())), preferred_element_type=F32)

    def cut(whole, k):
        return lax.dynamic_slice_in_dim(whole, (z ^ k) * 64, 64)

    near = [z ^ k for k in range(SIDE)]
    got = [unpacked(z_flip(packed(cut(state, k), factor), k)) for k in range(1, SIDE)]
    pieces = [cut(state, 0)] + [piece for piece, _ in got]
    factors = [factor] + [f for _, f in got]
    line = prefix(pieces, factors, near, SIDE)
    line_factor = between(factors, near, -1, SIDE)
    far = [x ^ k for k in range(1, SIDE)]
    lines = [unpacked(x_flip(packed(line, line_factor), k)) for k in range(1, SIDE)]
    entry = prefix([p for p, _ in lines], [f for _, f in lines], far, x)

    def entering(target):
        return prefix(pieces, factors, near, target) + between(factors, near, -1, target) * entry

    slices = [entering(z)] + [z_flip(entering(z ^ k).astype(BF), k) for k in range(1, SIDE)]

    queries = project(w_query).astype(BF)
    gates = project(w_gate).astype(BF).astype(F32)
    spread = cumul[:, None] - cumul[None, :]
    mask = jnp.arange(512)[:, None] >= jnp.arange(512)[None, :]
    weights = jnp.exp(jnp.where(mask, spread, -1e30))
    scores = lax.dot_general(queries, keys, (((1,), (1,)), ((), ())), preferred_element_type=F32)
    local = dot((scores * weights).astype(BF), values)

    whole = jnp.zeros((DK, DV), BF)
    for k in range(SIDE):
        whole = lax.dynamic_update_slice_in_dim(whole, slices[k].astype(BF), (z ^ k) * 64, 0)
    retained = local + jnp.exp(cumul)[:, None] * dot(queries, whole)
    center = retained - jnp.mean(retained, axis=-1, keepdims=True)
    variance = jnp.mean(center * center, axis=-1, keepdims=True)
    normed = center * lax.rsqrt(variance + 1e-5)
    hidden = (jax.nn.silu(gates) * normed).astype(BF)
    other = tp_swap(hidden)

    def partial(step):
        owner = (y + step) % SIDE
        mine = lax.dynamic_index_in_dim(w_own, owner, 1, keepdims=False)
        theirs = lax.dynamic_index_in_dim(w_other, owner, 1, keepdims=False)
        return dot(hidden, mine) + dot(other, theirs)

    opposite = partial(2).astype(BF)
    via_right, via_left = tp_shift(opposite[:256], 1), tp_shift(opposite[256:], -1)
    right, left = partial(1), partial(-1)
    low_right, top_left = tp_shift(right[256:].astype(BF), 1), tp_shift(left[:256].astype(BF), -1)
    top_right = tp_shift((right[:256] + via_right.astype(F32)).astype(BF), 1)
    low_left = tp_shift((left[256:] + via_left.astype(F32)).astype(BF), -1)
    own = partial(0)
    out_top = own[:256] + top_right.astype(F32) + top_left.astype(F32)
    out_low = own[256:] + low_right.astype(F32) + low_left.astype(F32)
    return jnp.concatenate([out_top, out_low]).astype(BF)


def solution(mesh):
    in_specs = (P("ctx", "tp"),) + (P(None, "tp"),) * 4 + (P("tp", None), P("tp", "ctx"))
    return jax.shard_map(
        shards, mesh=mesh, in_specs=in_specs, out_specs=P("ctx", "tp"), check_vma=False
    )
```

```python
import functools

import jax
import jax.numpy as jnp
from jax import lax
from jax.experimental import pallas as pl
from jax.experimental.pallas import tpu as pltpu
from jax.sharding import PartitionSpec as P

DK = 256
DV = 512
ROWS = 512
HALF = 256
WIDE = 512
SIDE = 4
CUT = DK // SIDE
MSG = CUT + 16
BF, F32 = jnp.bfloat16, jnp.float32
VM = pl.BlockSpec(memory_space=pltpu.VMEM)
SM = pl.BlockSpec(memory_space=pltpu.SMEM)
ANY = pl.BlockSpec(memory_space=pl.ANY)
HBM = pl.BlockSpec(memory_space=pltpu.HBM)


def tp_shift(value, step):
    return lax.ppermute(value, "tp", [(i, (i + 2 * step) % 8) for i in range(8)])


def tp_swap(value):
    return lax.ppermute(value, "tp", [(i, i ^ 1) for i in range(8)])


def z_flip(value, k):
    return lax.ppermute(value, "ctx", [(i, i ^ k) for i in range(16)])


def x_flip(value, k):
    return lax.ppermute(value, "ctx", [(i, i ^ (4 * k)) for i in range(16)])


def dot(a, b):
    return jnp.dot(a, b, preferred_element_type=F32)


def call(body, outs, in_specs, args, name, scratch=(), flops=0, moved=0, limit=16, out_specs=None, after=()):
    shapes = [jax.ShapeDtypeStruct(shape, dtype) for shape, dtype in outs]

    def whole(*refs):
        body(*refs[: len(args)], *refs[len(args) + len(after):])

    return pl.pallas_call(
        whole,
        out_shape=shapes,
        in_specs=list(in_specs) + [ANY] * len(after),
        out_specs=out_specs or [VM] * len(shapes),
        scratch_shapes=list(scratch),
        name=name,
        cost_estimate=pl.CostEstimate(flops=flops, bytes_accessed=moved, transcendentals=0),
        compiler_params=pltpu.CompilerParams(vmem_limit_bytes=limit * 1024 * 1024),
    )(*args, *after)


def project_body(owners, halves, n_weights, started, place, *refs):
    shards = []
    for half in halves:
        shards.append(jnp.concatenate([refs[0][...], refs[1][...]], axis=0) if half else refs[0][...])
        refs = refs[2 if half else 1:]
    weights, refs = refs[:n_weights], refs[n_weights:]
    sums, outs = (refs[:n_weights], refs[n_weights:]) if started else ([None] * n_weights, refs)
    for weight, before, out in zip(weights, sums, outs):
        total = None if before is None else before[...]
        for shard, owner in zip(shards, owners):
            rows = pl.ds(pl.multiple_of(place[owner] * WIDE, WIDE), WIDE)
            new = dot(shard, weight[rows, :])
            total = new if total is None else total + new
        out[...] = total


def project(place, owners, shards, weights, before, name, after=()):
    halves = [isinstance(s, tuple) for s in shards]
    flat = [p for s in shards for p in (s if isinstance(s, tuple) else (s,))]
    n = len(weights)
    widths = [w.shape[1] for w in weights]
    return call(
        functools.partial(project_body, owners, halves, n, before is not None),
        [((ROWS, width), F32) for width in widths],
        [SM] + [VM] * (len(flat) + n + (n if before else 0)),
        [place, *flat, *weights, *(before or [])],
        name,
        flops=2 * ROWS * WIDE * len(owners) * sum(widths),
        moved=WIDE * len(owners) * sum(widths) * 2,
        after=after,
    )


def tie(values, after, name):
    n = len(values)

    def body(*refs):
        pass

    return pl.pallas_call(
        body,
        out_shape=[jax.ShapeDtypeStruct(v.shape, v.dtype) for v in values],
        in_specs=[ANY] * (n + len(after)),
        out_specs=[ANY] * n,
        input_output_aliases={i: i for i in range(n)},
        name=name,
        compiler_params=pltpu.CompilerParams(vmem_limit_bytes=4 * 1024 * 1024),
    )(*values, *after)


def state_body(place, own0, own1, key_sum, value_sum, wk, wv, remain, factor, keys, values, mine, m1, m2, m3, state):
    x = jnp.concatenate([own0[...], own1[...]], axis=0)
    rows = pl.ds(pl.multiple_of(place[7] * WIDE, WIDE), WIDE)
    k = ((key_sum[...] + dot(x, wk[rows, :])) * DK ** (-0.5)).astype(BF)
    v = (value_sum[...] + dot(x, wv[rows, :])).astype(BF)
    keys[...] = k
    values[...] = v
    weighted = (k.astype(F32) * remain[...]).astype(BF)
    state[...] = lax.dot_general(weighted, v, (((0,), (0,)), ((), ())), preferred_element_type=F32)
    z = place[8]
    total = factor[...]
    high = total.astype(BF)
    rest = (total - high.astype(F32)).astype(BF)
    for i, ref in enumerate((mine, m1, m2, m3)):
        piece = state[pl.ds(pl.multiple_of((z ^ i) * CUT, CUT), CUT), :]
        if i == 0:
            ref[...] = piece
        else:
            ref[...] = jnp.concatenate(
                [piece.astype(BF), jnp.broadcast_to(high, (8, DV)), jnp.broadcast_to(rest, (8, DV))], axis=0
            )


def open_message(ref):
    ends = ref[CUT:, :].astype(F32)
    return ref[:CUT, :].astype(F32), ends[0:1] + ends[8:9]


def between(factors, sources, low, high):
    product = jnp.ones_like(factors[0])
    for factor, source in zip(factors, sources):
        product = product * jnp.where((source > low) & (source < high), factor, 1.0)
    return product


def prefix(pieces, factors, sources, target):
    total = jnp.zeros_like(pieces[0])
    for piece, source in zip(pieces, sources):
        weight = between(factors, sources, source, target)
        total = total + jnp.where(source < target, weight, 0.0) * piece
    return total


def line_of(place, mine, factor, messages):
    opened = [open_message(m) for m in messages]
    z = place[8]
    pieces = [mine[...]] + [piece for piece, _ in opened]
    factors = [factor[...]] + [f for _, f in opened]
    return pieces, factors, [z ^ k for k in range(SIDE)]


def line_body(place, mine, factor, m1, m2, m3, out):
    pieces, factors, sources = line_of(place, mine, factor, (m1, m2, m3))
    total = between(factors, sources, -1, SIDE)
    high = total.astype(BF)
    rest = (total - high.astype(F32)).astype(BF)
    piece = prefix(pieces, factors, sources, SIDE)
    out[...] = jnp.concatenate(
        [piece.astype(BF), jnp.broadcast_to(high, (8, DV)), jnp.broadcast_to(rest, (8, DV))], axis=0
    )


def entry_body(place, mine, factor, m1, m2, m3, n1, n2, n3, e0, e1, e2, e3):
    pieces, factors, sources = line_of(place, mine, factor, (m1, m2, m3))
    x, z = place[9], place[8]
    opened = [open_message(n) for n in (n1, n2, n3)]
    entry = prefix([p for p, _ in opened], [f for _, f in opened], [x ^ k for k in range(1, SIDE)], x)
    for k, ref in enumerate((e0, e1, e2, e3)):
        target = z ^ k
        whole = prefix(pieces, factors, sources, target) + between(factors, sources, -1, target) * entry
        ref[...] = whole.astype(BF)


def decay_body(rates, remain, decay, factor, mask):
    rows = lax.broadcasted_iota(jnp.int32, (ROWS, ROWS), 0)
    cols = lax.broadcasted_iota(jnp.int32, (ROWS, ROWS), 1)
    rate_row = jnp.broadcast_to(rates[...], (ROWS, ROWS))
    rate_col = jnp.sum(jnp.where(rows == cols, rate_row, 0.0), axis=1, keepdims=True)
    cumul_col = jnp.sum(jnp.where(rows >= cols, rate_row, 0.0), axis=1, keepdims=True)
    cumul_row = jnp.sum(jnp.where(rows <= cols, rate_col, 0.0), axis=0, keepdims=True)
    total = cumul_col[ROWS - 1:]
    remain[...] = jnp.exp(total - cumul_col)
    decay[...] = jnp.exp(cumul_col)
    factor[...] = jnp.broadcast_to(jnp.exp(total), (1, DV))
    mask[...] = jnp.exp(jnp.where(rows >= cols, cumul_col - cumul_row, -1e30))


def local_body(query_sum, keys, values, mask, queries, local):
    q = query_sum[...].astype(BF)
    queries[...] = q
    scores = lax.dot_general(q, keys[...], (((1,), (1,)), ((), ())), preferred_element_type=F32)
    local[...] = dot((scores * mask[...]).astype(BF), values[...])


def hidden_body(half, place, queries, e0, e1, e2, e3, local, decay, gate_sum, hidden, whole):
    z = place[8]
    rows = pl.ds(half * HALF, HALF)
    for k, ref in enumerate((e0, e1, e2, e3)):
        whole[pl.ds(pl.multiple_of((z ^ k) * CUT, CUT), CUT), :] = ref[...]
    retained = local[rows, :] + decay[rows, :] * dot(queries[rows, :], whole[...])
    center = retained - jnp.mean(retained, axis=-1, keepdims=True)
    variance = jnp.mean(center * center, axis=-1, keepdims=True)
    gate = gate_sum[rows, :].astype(BF).astype(F32)
    hidden[...] = (gate / (1.0 + jnp.exp(-gate)) * (center * lax.rsqrt(variance + 1e-5))).astype(BF)


def halve_body(before, after, top, low):
    top[...] = before[:HALF]
    low[...] = after[HALF:]


STEPS = (2, 1, -1, 0)


def pick_body(place, weight, given_far, given, given_own, kept_far, kept, kept_own, sems):
    core, y = place[10], place[11]
    copies = []
    for i, step in enumerate(STEPS):
        block = (y + step) % SIDE
        for j, (outs, which) in enumerate((((given_far, given, given_own), 1 - core), ((kept_far, kept, kept_own), core))):
            columns = pl.ds(pl.multiple_of((2 * block + which) * DV, DV), DV)
            out = (outs[0], outs[1].at[:, pl.ds(0, DV)], outs[1].at[:, pl.ds(DV, DV)], outs[2])[i]
            copy = pltpu.make_async_copy(weight.at[:, columns], out, sems.at[i, j])
            copy.start()
            copies.append(copy)
    for copy in copies:
        copy.wait()


def partial_body(n, *refs):
    hidden = jnp.concatenate([r[...] for r in refs[:n]], axis=0)
    other = jnp.concatenate([r[...] for r in refs[n: 2 * n]], axis=0)
    mine, theirs, outs = refs[2 * n], refs[2 * n + 1], refs[2 * n + 2:]
    total = dot(hidden, mine[...]) + dot(other, theirs[...])
    for i, out in enumerate(outs):
        rows, columns = (i % n) * HALF, (i // n) * DV
        out[...] = total[rows: rows + HALF, columns: columns + DV].astype(out.dtype)


def partial(hidden, other, mine, theirs, kinds, name, after=()):
    width, n = mine.shape[1], len(hidden)
    return call(
        functools.partial(partial_body, n),
        [((HALF, DV), kind) for kind in kinds],
        [VM] * (2 * n + 2),
        [*hidden, *other, mine, theirs],
        name,
        flops=4 * n * HALF * DV * width,
        moved=4 * DV * width,
        after=after,
    )


def own_body(h0, h1, o0, o1, mine, theirs, top, low, out_top, out_low):
    for h, o, come, out in ((h0, o0, top, out_top), (h1, o1, low, out_low)):
        out[...] = dot(h[...], mine[...]) + dot(o[...], theirs[...]) + come[...].astype(F32)


def final_body(own_top, own_low, top, low, out):
    out[:HALF, :] = (own_top[...] + top[...].astype(F32)).astype(BF)
    out[HALF:, :] = (own_low[...] + low[...].astype(F32)).astype(BF)


def added(mine, come):
    return (mine + come.astype(F32)).astype(BF)


def shards(tokens, w_query, w_key, w_value, w_gate, w_out, log_decay):
    ctx, tp = lax.axis_index("ctx"), lax.axis_index("tp")
    w_out = pltpu.with_memory_space_constraint(w_out, pltpu.HBM)
    x, z, y, core = ctx // SIDE, ctx % SIDE, tp // 2, tp % 2
    owners = [2 * ((y + step) % SIDE) + c for step in (0, -1, 1, 2) for c in (core, 1 - core)]
    place = jnp.stack([jnp.asarray(v, jnp.int32) for v in (*owners, z, x, core, y)])

    own_s = tp_swap(tokens)
    before, after = tp_shift(tokens, 1), tp_shift(tokens, -1)
    remain, decay, factor, mask = call(
        decay_body,
        [((ROWS, 1), F32)] * 2 + [((1, DV), F32), ((ROWS, ROWS), F32)],
        [VM],
        [log_decay],
        "decay",
        flops=ROWS * ROWS * 64,
    )
    given_far, given, given_own, kept_far, kept, kept_own = call(
        pick_body, [((DV, DV), BF), ((DV, 2 * DV), BF), ((DV, DV), BF)] * 2, [SM, HBM], [place, w_out], "pick",
        scratch=[pltpu.SemaphoreType.DMA((SIDE, 2))], moved=8 * DV * DV * 4,
    )
    theirs_far, theirs, theirs_own = tp_swap(given_far), tp_swap(given), tp_swap(given_own)

    kv = (w_key, w_value)
    sums = project(place, (0, 1), (tokens, own_s), kv, None, "kv_own", after=[kept_far])
    before, after = tie((before, after), [sums[0], mask], "tie")
    halves = call(
        halve_body, [((HALF, WIDE), BF)] * 2, [VM] * 2, [before, after], "halve", moved=ROWS * WIDE * 2,
    )
    before_s, after_s = tp_swap(before), tp_swap(after)
    across = (tp_shift(halves[0], 1), tp_shift(halves[1], -1))
    across_s = tuple(tp_swap(p) for p in across)
    sums = project(place, (2, 4, 3, 5), (before, after, before_s, after_s), kv, sums, "kv_near")
    sums = project(place, (6,), (across,), kv, sums, "kv_far")
    keys, values, mine, m1, m2, m3 = call(
        state_body,
        [((ROWS, DK), BF), ((ROWS, DV), BF), ((CUT, DV), F32)] + [((MSG, DV), BF)] * 3,
        [SM] + [VM] * 8,
        [place, *across_s, *sums, w_key, w_value, remain, factor],
        "state",
        scratch=[pltpu.VMEM((DK, DV), F32)],
        flops=2 * ROWS * (WIDE * (DK + DV) + DK * DV),
        moved=WIDE * (DK + DV) * 2,
    )
    messages = [z_flip(m, k + 1) for k, m in enumerate((m1, m2, m3))]

    everything = (tokens, own_s, before, after, before_s, after_s, across, across_s)
    order = (0, 1, 2, 4, 3, 5, 6, 7)
    (query_sum,) = project(place, order, everything, (w_query,), None, "queries", after=[keys])
    (line,) = call(
        line_body, [((MSG, DV), BF)], [SM] + [VM] * 5, [place, mine, factor, *messages], "line", moved=MSG * DV * 8,
        after=[query_sum],
    )
    lines = [x_flip(line, k) for k in range(1, SIDE)]
    (gate_sum,) = project(place, order, everything, (w_gate,), None, "gates", after=[line])
    e0, e1, e2, e3 = call(
        entry_body, [((CUT, DV), BF)] * 4, [SM] + [VM] * 8, [place, mine, factor, *messages, *lines], "entry",
        moved=MSG * DV * 16, after=[gate_sum],
    )
    queries, local = call(
        local_body,
        [((ROWS, DK), BF), ((ROWS, DV), F32)],
        [VM] * 4,
        [query_sum, keys, values, mask],
        "local",
        flops=2 * ROWS * ROWS * (DK + DV),
        moved=ROWS * DV * 4,
        after=[e0],
    )
    e1, e2, e3 = (z_flip(e, k + 1) for k, e in enumerate((e1, e2, e3)))
    hidden, other, far = [], [], []
    for half in range(2):
        (part,) = call(
            functools.partial(hidden_body, half), [((HALF, DV), BF)], [SM] + [VM] * 8,
            [place, queries, e0, e1, e2, e3, local, decay, gate_sum], f"hidden{half}",
            scratch=[pltpu.VMEM((DK, DV), BF)], flops=ROWS * DK * DV, moved=ROWS * DV * 4, after=hidden,
        )
        hidden.append(part)
        other.append(tp_swap(part))
    for half in range(2):
        far += partial(hidden[half: half + 1], other[half: half + 1], kept_far, theirs_far, (BF,), f"far{half}", after=far)
    via_right, via_left = tp_shift(far[0], 1), tp_shift(far[1], -1)
    r_top, r_low, l_top, l_low = partial(hidden, other, kept, theirs, (F32, BF, BF, F32), "beside", after=far)
    low_right, top_left = tp_shift(r_low, 1), tp_shift(l_top, -1)
    top_right, low_left = tp_shift(added(r_top, via_right), 1), tp_shift(added(l_low, via_left), -1)
    own = call(
        own_body, [((HALF, DV), F32)] * 2, [VM] * 8, [*hidden, *other, kept_own, theirs_own, top_left, low_right], "own",
        flops=4 * ROWS * DV * DV, moved=8 * DV * DV,
    )
    (out,) = call(
        final_body, [((ROWS, DV), BF)], [VM] * 4, [*own, top_right, low_left], "final", moved=ROWS * DV * 2,
    )
    return out


def solution(mesh):
    in_specs = (P("ctx", "tp"),) + (P(None, "tp"),) * 4 + (P("tp", None), P("tp", "ctx"))
    return jax.shard_map(
        shards, mesh=mesh, in_specs=in_specs, out_specs=P("ctx", "tp"), check_vma=False
    )
```

```python
import functools

import jax
import jax.numpy as jnp
from jax import lax
from jax.experimental import pallas as pl
from jax.experimental.pallas import tpu as pltpu
from jax.sharding import PartitionSpec as P

DK = 256
DV = 512
ROWS = 512
HALF = 256
WIDE = 512
SIDE = 4
CUT = DK // SIDE
MSG = CUT + 16
BF, F32 = jnp.bfloat16, jnp.float32
VM = pl.BlockSpec(memory_space=pltpu.VMEM)
ANY = pl.BlockSpec(memory_space=pl.ANY)
HBM = pl.BlockSpec(memory_space=pltpu.HBM)


def y_flip(value, k):
    return lax.ppermute(value, "tp", [(i, i ^ (2 * k)) for i in range(8)])


def tp_swap(value):
    return lax.ppermute(value, "tp", [(i, i ^ 1) for i in range(8)])


def z_flip(value, k):
    return lax.ppermute(value, "ctx", [(i, i ^ k) for i in range(16)])


def x_flip(value, k):
    return lax.ppermute(value, "ctx", [(i, i ^ (4 * k)) for i in range(16)])


def my(name):
    ctx, tp = lax.axis_index("ctx"), lax.axis_index("tp")
    return {"x": ctx // SIDE, "z": ctx % SIDE, "y": tp // 2, "core": tp % 2}[name]


def rows_of(step, same):
    core = my("core") if same else 1 - my("core")
    return pl.ds(pl.multiple_of((2 * (my("y") ^ step) + core) * WIDE, WIDE), WIDE)


def dot(a, b):
    return jnp.dot(a, b, preferred_element_type=F32)


def call(body, outs, in_specs, args, name, scratch=(), flops=0, moved=0, limit=16, out_specs=None, after=()):
    shapes = [jax.ShapeDtypeStruct(shape, dtype) for shape, dtype in outs]

    def whole(*refs):
        body(*refs[: len(args)], *refs[len(args) + len(after):])

    return pl.pallas_call(
        whole,
        out_shape=shapes,
        in_specs=list(in_specs) + [ANY] * len(after),
        out_specs=out_specs or [VM] * len(shapes),
        scratch_shapes=list(scratch),
        name=name,
        cost_estimate=pl.CostEstimate(flops=flops, bytes_accessed=moved, transcendentals=0),
        compiler_params=pltpu.CompilerParams(vmem_limit_bytes=limit * 1024 * 1024),
    )(*args, *after)


def join_body(top1, low1, top3, low3, near1, near3):
    for top, low, near in ((top1, low1, near1), (top3, low3, near3)):
        near[:HALF, :] = top[...]
        near[HALF:, :] = low[...]


def project_body(owners, halves, n_weights, started, gated, *refs):
    shards = []
    for half in halves:
        if half:
            shards.append(jnp.concatenate([refs[0][...], refs[1][...]], axis=0))
        else:
            shards.append(refs[0][...])
        refs = refs[2 if half else 1:]
    weights, refs = refs[:n_weights], refs[n_weights:]
    sums, outs = (refs[:n_weights], refs[n_weights:]) if started else ([None] * n_weights, refs)
    for weight, before, out in zip(weights, sums, outs):
        total = None if before is None else before[...]
        for shard, owner in zip(shards, owners):
            new = dot(shard, weight[rows_of(*owner), :])
            total = new if total is None else total + new
        out[...] = gate_of(total) if gated else total


def gate_of(total):
    gate = total.astype(BF).astype(F32)
    return gate / (1.0 + jnp.exp(-gate))


def project(owners, shards, weights, before, name, after=(), gated=False, hint=1):
    halves = [isinstance(s, tuple) for s in shards]
    flat = [p for s in shards for p in (s if isinstance(s, tuple) else (s,))]
    n = len(weights)
    widths = [w.shape[1] for w in weights]
    return call(
        functools.partial(project_body, owners, halves, n, before is not None, gated),
        [((ROWS, width), F32) for width in widths],
        [VM] * (len(flat) + n + (n if before else 0)),
        [*flat, *weights, *(before or [])],
        name,
        flops=2 * ROWS * WIDE * len(owners) * sum(widths) * hint + 1,
        moved=WIDE * len(owners) * sum(widths) * 2 * hint + 1,
        after=after,
    )


def tie(values, after, name):
    n = len(values)

    def body(*refs):
        pass

    return pl.pallas_call(
        body,
        out_shape=[jax.ShapeDtypeStruct(v.shape, v.dtype) for v in values],
        in_specs=[ANY] * (n + len(after)),
        out_specs=[ANY] * n,
        input_output_aliases={i: i for i in range(n)},
        name=name,
        compiler_params=pltpu.CompilerParams(vmem_limit_bytes=4 * 1024 * 1024),
    )(*values, *after)


def state_body(own0, own1, key_sum, value_sum, wk, wv, remain, factor, keys, values, mine, m1, m2, m3, state):
    x = jnp.concatenate([own0[...], own1[...]], axis=0)
    rows = rows_of(2, 0)
    k = ((key_sum[...] + dot(x, wk[rows, :])) * DK ** (-0.5)).astype(BF)
    v = (value_sum[...] + dot(x, wv[rows, :])).astype(BF)
    keys[...] = k
    values[...] = v
    weighted = (k.astype(F32) * remain[...]).astype(BF)
    state[...] = lax.dot_general(weighted, v, (((0,), (0,)), ((), ())), preferred_element_type=F32)
    z = my("z")
    total = factor[...]
    high = total.astype(BF)
    rest = (total - high.astype(F32)).astype(BF)
    for i, ref in enumerate((mine, m1, m2, m3)):
        piece = state[pl.ds(pl.multiple_of((z ^ i) * CUT, CUT), CUT), :]
        if i == 0:
            ref[...] = piece
        else:
            ref[...] = jnp.concatenate(
                [piece.astype(BF), jnp.broadcast_to(high, (8, DV)), jnp.broadcast_to(rest, (8, DV))], axis=0
            )


def open_message(ref):
    ends = ref[CUT:, :].astype(F32)
    return ref[:CUT, :].astype(F32), ends[0:1] + ends[8:9]


def between(factors, sources, low, high):
    product = jnp.ones_like(factors[0])
    for factor, source in zip(factors, sources):
        product = product * jnp.where((source > low) & (source < high), factor, 1.0)
    return product


def prefix(pieces, factors, sources, target):
    total = jnp.zeros_like(pieces[0])
    for piece, source in zip(pieces, sources):
        weight = between(factors, sources, source, target)
        total = total + jnp.where(source < target, weight, 0.0) * piece
    return total


def line_of(mine, factor, messages):
    opened = [open_message(m) for m in messages]
    z = my("z")
    pieces = [mine[...]] + [piece for piece, _ in opened]
    factors = [factor[...]] + [f for _, f in opened]
    return pieces, factors, [z ^ k for k in range(SIDE)]


def line_body(mine, factor, m1, m2, m3, out):
    pieces, factors, sources = line_of(mine, factor, (m1, m2, m3))
    total = between(factors, sources, -1, SIDE)
    high = total.astype(BF)
    rest = (total - high.astype(F32)).astype(BF)
    piece = prefix(pieces, factors, sources, SIDE)
    out[...] = jnp.concatenate(
        [piece.astype(BF), jnp.broadcast_to(high, (8, DV)), jnp.broadcast_to(rest, (8, DV))], axis=0
    )


def entry_body(mine, factor, m1, m2, m3, n1, n2, n3, e0, e1, e2, e3):
    pieces, factors, sources = line_of(mine, factor, (m1, m2, m3))
    x, z = my("x"), my("z")
    opened = [open_message(n) for n in (n1, n2, n3)]
    entry = prefix([p for p, _ in opened], [f for _, f in opened], [x ^ k for k in range(1, SIDE)], x)
    for k, ref in enumerate((e0, e1, e2, e3)):
        target = z ^ k
        whole = prefix(pieces, factors, sources, target) + between(factors, sources, -1, target) * entry
        ref[...] = whole.astype(BF)


def decay_body(rates, remain, decay, factor, mask):
    rows = lax.broadcasted_iota(jnp.int32, (ROWS, ROWS), 0)
    cols = lax.broadcasted_iota(jnp.int32, (ROWS, ROWS), 1)
    rate_row = jnp.broadcast_to(rates[...], (ROWS, ROWS))
    rate_col = jnp.sum(jnp.where(rows == cols, rate_row, 0.0), axis=1, keepdims=True)
    cumul_col = jnp.sum(jnp.where(rows >= cols, rate_row, 0.0), axis=1, keepdims=True)
    cumul_row = jnp.sum(jnp.where(rows <= cols, rate_col, 0.0), axis=0, keepdims=True)
    total = cumul_col[ROWS - 1:]
    remain[...] = jnp.exp(total - cumul_col)
    decay[...] = jnp.exp(cumul_col)
    factor[...] = jnp.broadcast_to(jnp.exp(total), (1, DV))
    mask[...] = jnp.exp(jnp.where(rows >= cols, cumul_col - cumul_row, -1e30))


def local_body(query_sum, keys, values, mask, queries, local):
    q = query_sum[...].astype(BF)
    queries[...] = q
    scores = lax.dot_general(q, keys[...], (((1,), (1,)), ((), ())), preferred_element_type=F32)
    local[...] = dot((scores * mask[...]).astype(BF), values[...])


def hidden_body(half, queries, e0, e1, e2, e3, local, decay, gates, hidden, whole):
    z = my("z")
    rows = pl.ds(half * HALF, HALF)
    for k, ref in enumerate((e0, e1, e2, e3)):
        whole[pl.ds(pl.multiple_of((z ^ k) * CUT, CUT), CUT), :] = ref[...]
    retained = local[rows, :] + decay[rows, :] * dot(queries[rows, :], whole[...])
    center = retained - jnp.mean(retained, axis=-1, keepdims=True)
    variance = jnp.mean(center * center, axis=-1, keepdims=True)
    hidden[...] = (gates[rows, :] * (center * lax.rsqrt(variance + 1e-5))).astype(BF)


def cut_body(tokens, top, low, sems):
    copies = [
        pltpu.make_async_copy(tokens.at[pl.ds(i * HALF, HALF), :], out, sems.at[i]) for i, out in enumerate((top, low))
    ]
    for copy in copies:
        copy.start()
    for copy in copies:
        copy.wait()


STEPS = (2, 1, 3, 0)


def pick_body(weight, given_far, given, given_own, kept_far, kept, kept_own, sems):
    core, y = my("core"), my("y")
    copies = []
    for i, step in enumerate(STEPS):
        block = y ^ step
        for j, (outs, which) in enumerate((((given_far, given, given_own), 1 - core), ((kept_far, kept, kept_own), core))):
            columns = pl.ds(pl.multiple_of((2 * block + which) * DV, DV), DV)
            out = (outs[0], outs[1].at[:, pl.ds(0, DV)], outs[1].at[:, pl.ds(DV, DV)], outs[2])[i]
            copy = pltpu.make_async_copy(weight.at[:, columns], out, sems.at[i, j])
            copy.start()
            copies.append(copy)
    for copy in copies:
        copy.wait()


def partial_body(n, *refs):
    hidden = jnp.concatenate([r[...] for r in refs[:n]], axis=0)
    other = jnp.concatenate([r[...] for r in refs[n: 2 * n]], axis=0)
    mine, theirs, outs = refs[2 * n], refs[2 * n + 1], refs[2 * n + 2:]
    total = dot(hidden, mine[...]) + dot(other, theirs[...])
    for i, out in enumerate(outs):
        rows, columns = (i % n) * HALF, (i // n) * DV
        out[...] = total[rows: rows + HALF, columns: columns + DV].astype(out.dtype)


def partial(hidden, other, mine, theirs, kinds, name, after=()):
    width, n = mine.shape[1], len(hidden)
    return call(
        functools.partial(partial_body, n),
        [((HALF, DV), kind) for kind in kinds],
        [VM] * (2 * n + 2),
        [*hidden, *other, mine, theirs],
        name,
        flops=4 * n * HALF * DV * width,
        moved=4 * DV * width,
        after=after,
    )


def own_body(h0, h1, o0, o1, mine, theirs, top, low, out_top, out_low):
    for h, o, come, out in ((h0, o0, top, out_top), (h1, o1, low, out_low)):
        out[...] = dot(h[...], mine[...]) + dot(o[...], theirs[...]) + come[...].astype(F32)


def final_body(own_top, own_low, top, low, out):
    out[:HALF, :] = (own_top[...] + top[...].astype(F32)).astype(BF)
    out[HALF:, :] = (own_low[...] + low[...].astype(F32)).astype(BF)


def added(mine, come):
    return (mine + come.astype(F32)).astype(BF)


def shards(tokens, w_query, w_key, w_value, w_gate, w_out, log_decay):
    w_out = pltpu.with_memory_space_constraint(w_out, pltpu.HBM)

    top, low = call(
        cut_body, [((HALF, WIDE), BF)] * 2, [ANY], [tokens], "cut", scratch=[pltpu.SemaphoreType.DMA((2,))],
        moved=ROWS * WIDE * 4,
    )
    a1, a3 = y_flip(top, 1), y_flip(low, 3)
    b1, b3 = y_flip(low, 1), y_flip(top, 3)
    own_s = tp_swap(tokens)
    remain, decay, factor, mask = call(
        decay_body,
        [((ROWS, 1), F32)] * 2 + [((1, DV), F32), ((ROWS, ROWS), F32)],
        [VM],
        [log_decay],
        "decay",
    )
    given_far, given, given_own, kept_far, kept, kept_own = call(
        pick_body, [((DV, DV), BF), ((DV, 2 * DV), BF), ((DV, DV), BF)] * 2, [HBM], [w_out], "pick",
        scratch=[pltpu.SemaphoreType.DMA((SIDE, 2))], moved=1,
    )
    kv = (w_key, w_value)
    sums = project(((0, 1), (0, 0)), (tokens, own_s), kv, None, "kv_own", hint=0)
    a1, a3 = tie((a1, a3), [kept_far, mask, sums[0]], "tie_a")
    c3, c1 = y_flip(a1, 3), y_flip(a3, 1)
    theirs_far, theirs, theirs_own = tp_swap(given_far), tp_swap(given), tp_swap(given_own)

    near1, near3 = call(join_body, [((ROWS, WIDE), BF)] * 2, [VM] * 4, [a1, b1, b3, a3], "join", moved=1)
    near1_s, near3_s = tp_swap(near1), tp_swap(near3)
    sums = project(((1, 1), (3, 1)), (near1, near3), kv, sums, "kv_near", hint=0)
    across = tie((c3, c1), sums[:1], "tie_c")
    across_s = tuple(tp_swap(p) for p in across)
    sums = project(((2, 1),), (tuple(across),), kv, sums, "kv_far", hint=10)
    sums = project(((1, 0), (3, 0)), (near1_s, near3_s), kv, sums, "kv_near_s", hint=0)
    keys, values, mine, m1, m2, m3 = call(
        state_body,
        [((ROWS, DK), BF), ((ROWS, DV), BF), ((CUT, DV), F32)] + [((MSG, DV), BF)] * 3,
        [VM] * 8,
        [*across_s, *sums, w_key, w_value, remain, factor],
        "state",
        scratch=[pltpu.VMEM((DK, DV), F32)],
        flops=2 * ROWS * (WIDE * (DK + DV) + DK * DV),
        moved=WIDE * (DK + DV) * 2,
    )
    messages = [z_flip(m, k + 1) for k, m in enumerate((m1, m2, m3))]

    everything = (tokens, own_s, near1, near3, near1_s, near3_s, tuple(across), across_s)
    order = ((0, 1), (0, 0), (1, 1), (3, 1), (1, 0), (3, 0), (2, 1), (2, 0))
    (query_sum,) = project(order, everything, (w_query,), None, "queries", after=[keys])
    (line,) = call(
        line_body, [((MSG, DV), BF)], [VM] * 5, [mine, factor, *messages], "line", moved=MSG * DV * 8,
        after=[query_sum],
    )
    lines = [x_flip(line, k) for k in range(1, SIDE)]
    (gates,) = project(order, everything, (w_gate,), None, "gates", after=[line], gated=True)
    e0, e1, e2, e3 = call(
        entry_body, [((CUT, DV), BF)] * 4, [VM] * 8, [mine, factor, *messages, *lines], "entry",
        moved=MSG * DV * 16, after=[gates],
    )
    queries, local = call(
        local_body,
        [((ROWS, DK), BF), ((ROWS, DV), F32)],
        [VM] * 4,
        [query_sum, keys, values, mask],
        "local",
        flops=2 * ROWS * ROWS * (DK + DV),
        moved=ROWS * DV * 4,
        after=[e0],
    )
    e1, e2, e3 = (z_flip(e, k + 1) for k, e in enumerate((e1, e2, e3)))
    hidden, other, far = [], [], []
    for half in range(2):
        (part,) = call(
            functools.partial(hidden_body, half), [((HALF, DV), BF)], [VM] * 8,
            [queries, e0, e1, e2, e3, local, decay, gates], f"hidden{half}",
            scratch=[pltpu.VMEM((DK, DV), BF)], flops=ROWS * DK * DV, moved=ROWS * DV * 4, after=hidden,
        )
        hidden.append(part)
        other.append(tp_swap(part))
    for half in range(2):
        far += partial(hidden[half: half + 1], other[half: half + 1], kept_far, theirs_far, (BF,), f"far{half}", after=far)
    via3, via1 = y_flip(far[0], 3), y_flip(far[1], 1)
    top1, low1, top3, low3 = partial(hidden, other, kept, theirs, (F32, BF, BF, F32), "beside", after=far)
    from1_low, from3_top = y_flip(low1, 1), y_flip(top3, 3)
    from1_top, from3_low = y_flip(added(top1, via3), 1), y_flip(added(low3, via1), 3)
    own = call(
        own_body, [((HALF, DV), F32)] * 2, [VM] * 8, [*hidden, *other, kept_own, theirs_own, from3_top, from1_low], "own",
        flops=4 * ROWS * DV * DV, moved=8 * DV * DV,
    )
    (out,) = call(
        final_body, [((ROWS, DV), BF)], [VM] * 4, [*own, from1_top, from3_low], "final", moved=ROWS * DV * 2,
    )
    return out


def solution(mesh):
    in_specs = (P("ctx", "tp"),) + (P(None, "tp"),) * 4 + (P("tp", None), P("tp", "ctx"))
    return jax.shard_map(
        shards, mesh=mesh, in_specs=in_specs, out_specs=P("ctx", "tp"), check_vma=False
    )
```

```python
import functools

import jax
import jax.numpy as jnp
from jax import lax
from jax.experimental import pallas as pl
from jax.experimental.pallas import tpu as pltpu
from jax.sharding import PartitionSpec as P

DK = 256
DV = 512
ROWS = 512
HALF = 256
WIDE = 512
SIDE = 4
CUT = DK // SIDE
MSG = CUT + 16
BF, F32 = jnp.bfloat16, jnp.float32
VM = pl.BlockSpec(memory_space=pltpu.VMEM)
ANY = pl.BlockSpec(memory_space=pl.ANY)
HBM = pl.BlockSpec(memory_space=pltpu.HBM)


def turn(k, core):
    return k ^ (2 * core) if k % 2 else k


def meet(k, core):
    return turn((0, 2, 3, 1)[k], core)


def y_flip(value, k):
    return lax.ppermute(value, "tp", [(i, i ^ (2 * turn(k, i % 2))) for i in range(8)])


def tp_swap(value):
    return lax.ppermute(value, "tp", [(i, i ^ 1) for i in range(8)])


def z_flip(value, k):
    return ctx_flip(value, k, 1)


def x_flip(value, k):
    return ctx_flip(value, k, 4)


def ctx_flip(value, k, unit):
    pairs = [(8 * i + j, 8 * (i ^ (unit * meet(k, j % 2))) + j) for i in range(16) for j in range(8)]
    return lax.ppermute(value, ("ctx", "tp"), pairs)


def my(name):
    ctx, tp = lax.axis_index("ctx"), lax.axis_index("tp")
    return {"x": ctx // SIDE, "z": ctx % SIDE, "y": tp // 2, "core": tp % 2}[name]


def rows_of(step, same):
    core = my("core") if same else 1 - my("core")
    return pl.ds(pl.multiple_of((2 * (my("y") ^ turn(step, core)) + core) * WIDE, WIDE), WIDE)


def dot(a, b):
    return jnp.dot(a, b, preferred_element_type=F32)


def call(body, outs, in_specs, args, name, scratch=(), flops=0, moved=0, limit=16, out_specs=None, after=()):
    shapes = [jax.ShapeDtypeStruct(shape, dtype) for shape, dtype in outs]

    def whole(*refs):
        body(*refs[: len(args)], *refs[len(args) + len(after):])

    return pl.pallas_call(
        whole,
        out_shape=shapes,
        in_specs=list(in_specs) + [ANY] * len(after),
        out_specs=out_specs or [VM] * len(shapes),
        scratch_shapes=list(scratch),
        name=name,
        cost_estimate=pl.CostEstimate(flops=flops, bytes_accessed=moved, transcendentals=0),
        compiler_params=pltpu.CompilerParams(vmem_limit_bytes=limit * 1024 * 1024),
    )(*args, *after)


def join_body(top1, low1, top3, low3, near1, near3):
    for top, low, near in ((top1, low1, near1), (top3, low3, near3)):
        near[:HALF, :] = top[...]
        near[HALF:, :] = low[...]


def project_body(owners, halves, n_weights, started, gated, *refs):
    shards = []
    for half in halves:
        if half:
            shards.append(jnp.concatenate([refs[0][...], refs[1][...]], axis=0))
        else:
            shards.append(refs[0][...])
        refs = refs[2 if half else 1:]
    weights, refs = refs[:n_weights], refs[n_weights:]
    sums, outs = (refs[:n_weights], refs[n_weights:]) if started else ([None] * n_weights, refs)
    for weight, before, out in zip(weights, sums, outs):
        total = None if before is None else before[...]
        for shard, owner in zip(shards, owners):
            new = dot(shard, weight[rows_of(*owner), :])
            total = new if total is None else total + new
        out[...] = gate_of(total) if gated else total


def gate_of(total):
    gate = total.astype(BF).astype(F32)
    return gate / (1.0 + jnp.exp(-gate))


def project(owners, shards, weights, before, name, after=(), gated=False, hint=1):
    halves = [isinstance(s, tuple) for s in shards]
    flat = [p for s in shards for p in (s if isinstance(s, tuple) else (s,))]
    n = len(weights)
    widths = [w.shape[1] for w in weights]
    return call(
        functools.partial(project_body, owners, halves, n, before is not None, gated),
        [((ROWS, width), F32) for width in widths],
        [VM] * (len(flat) + n + (n if before else 0)),
        [*flat, *weights, *(before or [])],
        name,
        flops=2 * ROWS * WIDE * len(owners) * sum(widths) * hint + 1,
        moved=WIDE * len(owners) * sum(widths) * 2 * hint + 1,
        after=after,
    )


def tie(values, after, name):
    n = len(values)

    def body(*refs):
        pass

    return pl.pallas_call(
        body,
        out_shape=[jax.ShapeDtypeStruct(v.shape, v.dtype) for v in values],
        in_specs=[ANY] * (n + len(after)),
        out_specs=[ANY] * n,
        input_output_aliases={i: i for i in range(n)},
        name=name,
        compiler_params=pltpu.CompilerParams(vmem_limit_bytes=4 * 1024 * 1024),
    )(*values, *after)


def state_body(own0, own1, key_sum, value_sum, wk, wv, remain, factor, keys, values, mine, m1, m2, m3, state):
    x = jnp.concatenate([own0[...], own1[...]], axis=0)
    rows = rows_of(2, 0)
    k = ((key_sum[...] + dot(x, wk[rows, :])) * DK ** (-0.5)).astype(BF)
    v = (value_sum[...] + dot(x, wv[rows, :])).astype(BF)
    keys[...] = k
    values[...] = v
    weighted = (k.astype(F32) * remain[...]).astype(BF)
    state[...] = lax.dot_general(weighted, v, (((0,), (0,)), ((), ())), preferred_element_type=F32)
    z = my("z")
    total = factor[...]
    high = total.astype(BF)
    rest = (total - high.astype(F32)).astype(BF)
    for i, ref in enumerate((mine, m1, m2, m3)):
        piece = state[pl.ds(pl.multiple_of((z ^ meet(i, my("core"))) * CUT, CUT), CUT), :]
        if i == 0:
            ref[...] = piece
        else:
            ref[...] = jnp.concatenate(
                [piece.astype(BF), jnp.broadcast_to(high, (8, DV)), jnp.broadcast_to(rest, (8, DV))], axis=0
            )


def open_message(ref):
    ends = ref[CUT:, :].astype(F32)
    return ref[:CUT, :].astype(F32), ends[0:1] + ends[8:9]


def between(factors, sources, low, high):
    product = jnp.ones_like(factors[0])
    for factor, source in zip(factors, sources):
        product = product * jnp.where((source > low) & (source < high), factor, 1.0)
    return product


def prefix(pieces, factors, sources, target):
    total = jnp.zeros_like(pieces[0])
    for piece, source in zip(pieces, sources):
        weight = between(factors, sources, source, target)
        total = total + jnp.where(source < target, weight, 0.0) * piece
    return total


def line_of(mine, factor, messages):
    opened = [open_message(m) for m in messages]
    z = my("z")
    pieces = [mine[...]] + [piece for piece, _ in opened]
    factors = [factor[...]] + [f for _, f in opened]
    return pieces, factors, [z ^ meet(k, my("core")) for k in range(SIDE)]


def line_body(mine, factor, m1, m2, m3, out):
    pieces, factors, sources = line_of(mine, factor, (m1, m2, m3))
    total = between(factors, sources, -1, SIDE)
    high = total.astype(BF)
    rest = (total - high.astype(F32)).astype(BF)
    piece = prefix(pieces, factors, sources, SIDE)
    out[...] = jnp.concatenate(
        [piece.astype(BF), jnp.broadcast_to(high, (8, DV)), jnp.broadcast_to(rest, (8, DV))], axis=0
    )


def entry_body(mine, factor, m1, m2, m3, n1, n2, n3, e0, e1, e2, e3):
    pieces, factors, sources = line_of(mine, factor, (m1, m2, m3))
    x, z = my("x"), my("z")
    opened = [open_message(n) for n in (n1, n2, n3)]
    entry = prefix([p for p, _ in opened], [f for _, f in opened], [x ^ meet(k, my("core")) for k in range(1, SIDE)], x)
    for k, ref in enumerate((e0, e1, e2, e3)):
        target = z ^ meet(k, my("core"))
        whole = prefix(pieces, factors, sources, target) + between(factors, sources, -1, target) * entry
        ref[...] = whole.astype(BF)


def decay_body(rates, remain, decay, factor, mask):
    rows = lax.broadcasted_iota(jnp.int32, (ROWS, ROWS), 0)
    cols = lax.broadcasted_iota(jnp.int32, (ROWS, ROWS), 1)
    rate_row = jnp.broadcast_to(rates[...], (ROWS, ROWS))
    rate_col = jnp.sum(jnp.where(rows == cols, rate_row, 0.0), axis=1, keepdims=True)
    cumul_col = jnp.sum(jnp.where(rows >= cols, rate_row, 0.0), axis=1, keepdims=True)
    cumul_row = jnp.sum(jnp.where(rows <= cols, rate_col, 0.0), axis=0, keepdims=True)
    total = cumul_col[ROWS - 1:]
    remain[...] = jnp.exp(total - cumul_col)
    decay[...] = jnp.exp(cumul_col)
    factor[...] = jnp.broadcast_to(jnp.exp(total), (1, DV))
    mask[...] = jnp.exp(jnp.where(rows >= cols, cumul_col - cumul_row, -1e30))


def local_body(query_sum, keys, values, mask, queries, local):
    q = query_sum[...].astype(BF)
    queries[...] = q
    scores = lax.dot_general(q, keys[...], (((1,), (1,)), ((), ())), preferred_element_type=F32)
    local[...] = dot((scores * mask[...]).astype(BF), values[...])


def hidden_body(half, queries, e0, e1, e2, e3, local, decay, gates, hidden, whole):
    z = my("z")
    rows = pl.ds(half * HALF, HALF)
    for k, ref in enumerate((e0, e1, e2, e3)):
        whole[pl.ds(pl.multiple_of((z ^ meet(k, my("core"))) * CUT, CUT), CUT), :] = ref[...]
    retained = local[rows, :] + decay[rows, :] * dot(queries[rows, :], whole[...])
    center = retained - jnp.mean(retained, axis=-1, keepdims=True)
    variance = jnp.mean(center * center, axis=-1, keepdims=True)
    hidden[...] = (gates[rows, :] * (center * lax.rsqrt(variance + 1e-5))).astype(BF)


def cut_body(tokens, top, low, sems):
    copies = [
        pltpu.make_async_copy(tokens.at[pl.ds(i * HALF, HALF), :], out, sems.at[i]) for i, out in enumerate((top, low))
    ]
    for copy in copies:
        copy.start()
    for copy in copies:
        copy.wait()


STEPS = (2, 1, 3, 0)


def pick_body(weight, given_far, given, kept_far, kept, sems):
    core, y = my("core"), my("y")
    copies = []
    for i, step in enumerate(STEPS):
        for j, (outs, which) in enumerate((((given_far, given), 1 - core), ((kept_far, kept), core))):
            block = y ^ turn(step, which)
            columns = pl.ds(pl.multiple_of((2 * block + which) * DV, DV), DV)
            out = outs[0] if i == 0 else outs[1].at[:, pl.ds((i - 1) * DV, DV)]
            copy = pltpu.make_async_copy(weight.at[:, columns], out, sems.at[i, j])
            copy.start()
            copies.append(copy)
    for copy in copies:
        copy.wait()


def partial_body(n, *refs):
    hidden = jnp.concatenate([r[...] for r in refs[:n]], axis=0)
    other = jnp.concatenate([r[...] for r in refs[n: 2 * n]], axis=0)
    mine, theirs, outs = refs[2 * n], refs[2 * n + 1], refs[2 * n + 2:]
    columns = pl.ds(0, len(outs) // n * DV)
    total = dot(hidden, mine[:, columns]) + dot(other, theirs[:, columns])
    for i, out in enumerate(outs):
        rows, columns = (i % n) * HALF, (i // n) * DV
        out[...] = total[rows: rows + HALF, columns: columns + DV].astype(out.dtype)


def partial(hidden, other, mine, theirs, kinds, name, after=()):
    n = len(hidden)
    width = len(kinds) // n * DV
    return call(
        functools.partial(partial_body, n),
        [((HALF, DV), kind) for kind in kinds],
        [VM] * (2 * n + 2),
        [*hidden, *other, mine, theirs],
        name,
        flops=4 * n * HALF * DV * width,
        moved=4 * DV * width,
        after=after,
    )


def own_body(h0, h1, o0, o1, mine, theirs, top, low, out_top, out_low):
    columns = pl.ds(2 * DV, DV)
    for h, o, come, out in ((h0, o0, top, out_top), (h1, o1, low, out_low)):
        out[...] = dot(h[...], mine[:, columns]) + dot(o[...], theirs[:, columns]) + come[...].astype(F32)


def final_body(own_top, own_low, top, low, out):
    out[:HALF, :] = (own_top[...] + top[...].astype(F32)).astype(BF)
    out[HALF:, :] = (own_low[...] + low[...].astype(F32)).astype(BF)


def added(mine, come):
    return (mine + come.astype(F32)).astype(BF)


def shards(tokens, w_query, w_key, w_value, w_gate, w_out, log_decay):
    w_out = pltpu.with_memory_space_constraint(w_out, pltpu.HBM)

    top, low = call(
        cut_body, [((HALF, WIDE), BF)] * 2, [ANY], [tokens], "cut", scratch=[pltpu.SemaphoreType.DMA((2,))],
        moved=ROWS * WIDE * 4,
    )
    a1, a3 = y_flip(top, 1), y_flip(low, 3)
    b1, b3 = y_flip(low, 1), y_flip(top, 3)
    own_s = tp_swap(tokens)
    remain, decay, factor, mask = call(
        decay_body,
        [((ROWS, 1), F32)] * 2 + [((1, DV), F32), ((ROWS, ROWS), F32)],
        [VM],
        [log_decay],
        "decay",
    )
    given_far, given, kept_far, kept = call(
        pick_body, [((DV, DV), BF), ((DV, 3 * DV), BF)] * 2, [HBM], [w_out], "pick",
        scratch=[pltpu.SemaphoreType.DMA((SIDE, 2))], moved=1,
    )
    kv = (w_key, w_value)
    sums = project(((0, 1), (0, 0)), (tokens, own_s), kv, None, "kv_own", hint=0)
    a1, a3 = tie((a1, a3), [kept_far, mask, sums[0]], "tie_a")
    c3, c1 = y_flip(a1, 3), y_flip(a3, 1)
    theirs_far, theirs = tp_swap(given_far), tp_swap(given)

    near1, near3 = call(join_body, [((ROWS, WIDE), BF)] * 2, [VM] * 4, [a1, b1, b3, a3], "join", moved=1)
    near1_s, near3_s = tp_swap(near1), tp_swap(near3)
    sums = project(((1, 1), (3, 1)), (near1, near3), kv, sums, "kv_near", hint=0)
    across = tie((c3, c1), sums[:1], "tie_c")
    across_s = tuple(tp_swap(p) for p in across)
    sums = project(((2, 1),), (tuple(across),), kv, sums, "kv_far", hint=10)
    sums = project(((1, 0), (3, 0)), (near1_s, near3_s), kv, sums, "kv_near_s", hint=0)
    keys, values, mine, m1, m2, m3 = call(
        state_body,
        [((ROWS, DK), BF), ((ROWS, DV), BF), ((CUT, DV), F32)] + [((MSG, DV), BF)] * 3,
        [VM] * 8,
        [*across_s, *sums, w_key, w_value, remain, factor],
        "state",
        scratch=[pltpu.VMEM((DK, DV), F32)],
        flops=2 * ROWS * (WIDE * (DK + DV) + DK * DV),
        moved=WIDE * (DK + DV) * 2,
    )
    messages = [z_flip(m, k + 1) for k, m in enumerate((m1, m2, m3))]

    everything = (tokens, own_s, near1, near3, near1_s, near3_s, tuple(across), across_s)
    order = ((0, 1), (0, 0), (1, 1), (3, 1), (1, 0), (3, 0), (2, 1), (2, 0))
    (query_sum,) = project(order, everything, (w_query,), None, "queries", after=[keys])
    (line,) = call(
        line_body, [((MSG, DV), BF)], [VM] * 5, [mine, factor, *messages], "line", moved=MSG * DV * 8,
        after=[query_sum],
    )
    lines = [x_flip(line, k) for k in range(1, SIDE)]
    (gates,) = project(order, everything, (w_gate,), None, "gates", after=[line], gated=True)
    e0, e1, e2, e3 = call(
        entry_body, [((CUT, DV), BF)] * 4, [VM] * 8, [mine, factor, *messages, *lines], "entry",
        moved=MSG * DV * 16, after=[gates],
    )
    queries, local = call(
        local_body,
        [((ROWS, DK), BF), ((ROWS, DV), F32)],
        [VM] * 4,
        [query_sum, keys, values, mask],
        "local",
        flops=2 * ROWS * ROWS * (DK + DV),
        moved=ROWS * DV * 4,
        after=[e0],
    )
    e1, e2, e3 = (z_flip(e, k + 1) for k, e in enumerate((e1, e2, e3)))
    hidden, other, far = [], [], []
    for half in range(2):
        (part,) = call(
            functools.partial(hidden_body, half), [((HALF, DV), BF)], [VM] * 8,
            [queries, e0, e1, e2, e3, local, decay, gates], f"hidden{half}",
            scratch=[pltpu.VMEM((DK, DV), BF)], flops=ROWS * DK * DV, moved=ROWS * DV * 4, after=hidden,
        )
        hidden.append(part)
        other.append(tp_swap(part))
    for half in range(2):
        far += partial(hidden[half: half + 1], other[half: half + 1], kept_far, theirs_far, (BF,), f"far{half}", after=far)
    via3, via1 = y_flip(far[0], 3), y_flip(far[1], 1)
    top1, low1, top3, low3 = partial(hidden, other, kept, theirs, (F32, BF, BF, F32), "beside", after=far)
    from1_low, from3_top = y_flip(low1, 1), y_flip(top3, 3)
    from1_top, from3_low = y_flip(added(top1, via3), 1), y_flip(added(low3, via1), 3)
    own = call(
        own_body, [((HALF, DV), F32)] * 2, [VM] * 8, [*hidden, *other, kept, theirs, from3_top, from1_low], "own",
        flops=4 * ROWS * DV * DV, moved=8 * DV * DV,
    )
    (out,) = call(
        final_body, [((ROWS, DV), BF)], [VM] * 4, [*own, from1_top, from3_low], "final", moved=ROWS * DV * 2,
    )
    return out


def solution(mesh):
    in_specs = (P("ctx", "tp"),) + (P(None, "tp"),) * 4 + (P("tp", None), P("tp", "ctx"))
    return jax.shard_map(
        shards, mesh=mesh, in_specs=in_specs, out_specs=P("ctx", "tp"), check_vma=False
    )
```

```python
import functools

import jax
import jax.numpy as jnp
from jax import lax
from jax.experimental import pallas as pl
from jax.experimental.pallas import tpu as pltpu
from jax.sharding import PartitionSpec as P

DK = 256
DV = 512
ROWS = 512
HALF = 256
WIDE = 512
SIDE = 4
CUT = DK // SIDE
MSG = CUT + 16
BF, F32 = jnp.bfloat16, jnp.float32
VM = pl.BlockSpec(memory_space=pltpu.VMEM)
ANY = pl.BlockSpec(memory_space=pl.ANY)
HBM = pl.BlockSpec(memory_space=pltpu.HBM)


def turn(k, core):
    return k ^ (2 * (1 - core)) if k % 2 else k


def meet(k, core, order):
    return turn(order[k], core)


Z_ORDER, X_ORDER = (0, 2, 1, 3), (0, 2, 1, 3)


def y_flip(value, k):
    return lax.ppermute(value, "tp", [(i, i ^ (2 * turn(k, i % 2))) for i in range(8)])


def tp_swap(value):
    return lax.ppermute(value, "tp", [(i, i ^ 1) for i in range(8)])


def z_flip(value, k):
    return ctx_flip(value, k, 1)


def x_flip(value, k):
    return ctx_flip(value, k, 4)


def ctx_flip(value, k, unit):
    pairs = [(8 * i + j, 8 * (i ^ (unit * meet(k, j % 2, Z_ORDER if unit == 1 else X_ORDER))) + j) for i in range(16) for j in range(8)]
    return lax.ppermute(value, ("ctx", "tp"), pairs)


def my(name):
    ctx, tp = lax.axis_index("ctx"), lax.axis_index("tp")
    return {"x": ctx // SIDE, "z": ctx % SIDE, "y": tp // 2, "core": tp % 2}[name]


def rows_of(step, same):
    core = my("core") if same else 1 - my("core")
    return pl.ds(pl.multiple_of((2 * (my("y") ^ turn(step, core)) + core) * WIDE, WIDE), WIDE)


def dot(a, b):
    return jnp.dot(a, b, preferred_element_type=F32)


def call(body, outs, in_specs, args, name, scratch=(), flops=0, moved=0, limit=16, out_specs=None, after=()):
    shapes = [jax.ShapeDtypeStruct(shape, dtype) for shape, dtype in outs]

    def whole(*refs):
        body(*refs[: len(args)], *refs[len(args) + len(after):])

    return pl.pallas_call(
        whole,
        out_shape=shapes,
        in_specs=list(in_specs) + [ANY] * len(after),
        out_specs=out_specs or [VM] * len(shapes),
        scratch_shapes=list(scratch),
        name=name,
        cost_estimate=pl.CostEstimate(flops=flops, bytes_accessed=moved, transcendentals=0),
        compiler_params=pltpu.CompilerParams(vmem_limit_bytes=limit * 1024 * 1024),
    )(*args, *after)


def join_body(top1, low1, top3, low3, near1, near3):
    for top, low, near in ((top1, low1, near1), (top3, low3, near3)):
        near[:HALF, :] = top[...]
        near[HALF:, :] = low[...]


def project_body(owners, halves, n_weights, started, gated, *refs):
    shards = []
    for half in halves:
        if half:
            shards.append(jnp.concatenate([refs[0][...], refs[1][...]], axis=0))
        else:
            shards.append(refs[0][...])
        refs = refs[2 if half else 1:]
    weights, refs = refs[:n_weights], refs[n_weights:]
    sums, outs = (refs[:n_weights], refs[n_weights:]) if started else ([None] * n_weights, refs)
    for weight, before, out in zip(weights, sums, outs):
        total = None if before is None else before[...]
        for shard, owner in zip(shards, owners):
            new = dot(shard, weight[rows_of(*owner), :])
            total = new if total is None else total + new
        out[...] = gate_of(total) if gated else total


def gate_of(total):
    gate = total.astype(BF).astype(F32)
    return gate / (1.0 + jnp.exp(-gate))


def project(owners, shards, weights, before, name, after=(), gated=False, hint=1):
    halves = [isinstance(s, tuple) for s in shards]
    flat = [p for s in shards for p in (s if isinstance(s, tuple) else (s,))]
    n = len(weights)
    widths = [w.shape[1] for w in weights]
    return call(
        functools.partial(project_body, owners, halves, n, before is not None, gated),
        [((ROWS, width), F32) for width in widths],
        [VM] * (len(flat) + n + (n if before else 0)),
        [*flat, *weights, *(before or [])],
        name,
        flops=2 * ROWS * WIDE * len(owners) * sum(widths) * hint + 1,
        moved=WIDE * len(owners) * sum(widths) * 2 * hint + 1,
        after=after,
    )


def tie(values, after, name):
    n = len(values)

    def body(*refs):
        pass

    return pl.pallas_call(
        body,
        out_shape=[jax.ShapeDtypeStruct(v.shape, v.dtype) for v in values],
        in_specs=[ANY] * (n + len(after)),
        out_specs=[ANY] * n,
        input_output_aliases={i: i for i in range(n)},
        name=name,
        compiler_params=pltpu.CompilerParams(vmem_limit_bytes=4 * 1024 * 1024),
    )(*values, *after)


def state_body(own0, own1, key_sum, value_sum, wk, wv, remain, factor, keys, values, mine, m1, m2, m3, state):
    x = jnp.concatenate([own0[...], own1[...]], axis=0)
    rows = rows_of(2, 0)
    k = ((key_sum[...] + dot(x, wk[rows, :])) * DK ** (-0.5)).astype(BF)
    v = (value_sum[...] + dot(x, wv[rows, :])).astype(BF)
    keys[...] = k
    values[...] = v
    weighted = (k.astype(F32) * remain[...]).astype(BF)
    state[...] = lax.dot_general(weighted, v, (((0,), (0,)), ((), ())), preferred_element_type=F32)
    z = my("z")
    total = factor[...]
    high = total.astype(BF)
    rest = (total - high.astype(F32)).astype(BF)
    for i, ref in enumerate((mine, m1, m2, m3)):
        piece = state[pl.ds(pl.multiple_of((z ^ meet(i, my("core"), Z_ORDER)) * CUT, CUT), CUT), :]
        if i == 0:
            ref[...] = piece
        else:
            ref[...] = jnp.concatenate(
                [piece.astype(BF), jnp.broadcast_to(high, (8, DV)), jnp.broadcast_to(rest, (8, DV))], axis=0
            )


def open_message(ref):
    ends = ref[CUT:, :].astype(F32)
    return ref[:CUT, :].astype(F32), ends[0:1] + ends[8:9]


def between(factors, sources, low, high):
    product = jnp.ones_like(factors[0])
    for factor, source in zip(factors, sources):
        product = product * jnp.where((source > low) & (source < high), factor, 1.0)
    return product


def prefix(pieces, factors, sources, target):
    total = jnp.zeros_like(pieces[0])
    for piece, source in zip(pieces, sources):
        weight = between(factors, sources, source, target)
        total = total + jnp.where(source < target, weight, 0.0) * piece
    return total


def line_of(mine, factor, messages):
    opened = [open_message(m) for m in messages]
    z = my("z")
    pieces = [mine[...]] + [piece for piece, _ in opened]
    factors = [factor[...]] + [f for _, f in opened]
    return pieces, factors, [z ^ meet(k, my("core"), Z_ORDER) for k in range(SIDE)]


def line_body(mine, factor, m1, m2, m3, out):
    pieces, factors, sources = line_of(mine, factor, (m1, m2, m3))
    total = between(factors, sources, -1, SIDE)
    high = total.astype(BF)
    rest = (total - high.astype(F32)).astype(BF)
    piece = prefix(pieces, factors, sources, SIDE)
    out[...] = jnp.concatenate(
        [piece.astype(BF), jnp.broadcast_to(high, (8, DV)), jnp.broadcast_to(rest, (8, DV))], axis=0
    )


def entry_body(mine, factor, m1, m2, m3, n1, n2, n3, e0, e1, e2, e3):
    pieces, factors, sources = line_of(mine, factor, (m1, m2, m3))
    x, z = my("x"), my("z")
    opened = [open_message(n) for n in (n1, n2, n3)]
    entry = prefix([p for p, _ in opened], [f for _, f in opened], [x ^ meet(k, my("core"), X_ORDER) for k in range(1, SIDE)], x)
    for k, ref in enumerate((e0, e1, e2, e3)):
        target = z ^ meet(k, my("core"), Z_ORDER)
        whole = prefix(pieces, factors, sources, target) + between(factors, sources, -1, target) * entry
        ref[...] = whole.astype(BF)


def decay_body(rates, remain, decay, factor, mask):
    rows = lax.broadcasted_iota(jnp.int32, (ROWS, ROWS), 0)
    cols = lax.broadcasted_iota(jnp.int32, (ROWS, ROWS), 1)
    rate_row = jnp.broadcast_to(rates[...], (ROWS, ROWS))
    rate_col = jnp.sum(jnp.where(rows == cols, rate_row, 0.0), axis=1, keepdims=True)
    cumul_col = jnp.sum(jnp.where(rows >= cols, rate_row, 0.0), axis=1, keepdims=True)
    cumul_row = jnp.sum(jnp.where(rows <= cols, rate_col, 0.0), axis=0, keepdims=True)
    total = cumul_col[ROWS - 1:]
    remain[...] = jnp.exp(total - cumul_col)
    decay[...] = jnp.exp(cumul_col)
    factor[...] = jnp.broadcast_to(jnp.exp(total), (1, DV))
    mask[...] = jnp.exp(jnp.where(rows >= cols, cumul_col - cumul_row, -1e30))


def local_body(query_sum, keys, values, mask, queries, local):
    q = query_sum[...].astype(BF)
    queries[...] = q
    scores = lax.dot_general(q, keys[...], (((1,), (1,)), ((), ())), preferred_element_type=F32)
    local[...] = dot((scores * mask[...]).astype(BF), values[...])


def hidden_body(half, queries, e0, e1, e2, e3, local, decay, gates, hidden, whole):
    z = my("z")
    rows = pl.ds(half * HALF, HALF)
    for k, ref in enumerate((e0, e1, e2, e3)):
        whole[pl.ds(pl.multiple_of((z ^ meet(k, my("core"), Z_ORDER)) * CUT, CUT), CUT), :] = ref[...]
    retained = local[rows, :] + decay[rows, :] * dot(queries[rows, :], whole[...])
    center = retained - jnp.mean(retained, axis=-1, keepdims=True)
    variance = jnp.mean(center * center, axis=-1, keepdims=True)
    hidden[...] = (gates[rows, :] * (center * lax.rsqrt(variance + 1e-5))).astype(BF)


def cut_body(tokens, top, low, sems):
    copies = [
        pltpu.make_async_copy(tokens.at[pl.ds(i * HALF, HALF), :], out, sems.at[i]) for i, out in enumerate((top, low))
    ]
    for copy in copies:
        copy.start()
    for copy in copies:
        copy.wait()


STEPS = (2, 1, 3, 0)


def pick_body(weight, given_far, given, kept_far, kept, sems):
    core, y = my("core"), my("y")
    copies = []
    for i, step in enumerate(STEPS):
        for j, (outs, which) in enumerate((((given_far, given), 1 - core), ((kept_far, kept), core))):
            block = y ^ turn(step, which)
            columns = pl.ds(pl.multiple_of((2 * block + which) * DV, DV), DV)
            out = outs[0] if i == 0 else outs[1].at[:, pl.ds((i - 1) * DV, DV)]
            copy = pltpu.make_async_copy(weight.at[:, columns], out, sems.at[i, j])
            copy.start()
            copies.append(copy)
    for copy in copies:
        copy.wait()


def partial_body(n, *refs):
    hidden = jnp.concatenate([r[...] for r in refs[:n]], axis=0)
    other = jnp.concatenate([r[...] for r in refs[n: 2 * n]], axis=0)
    mine, theirs, outs = refs[2 * n], refs[2 * n + 1], refs[2 * n + 2:]
    columns = pl.ds(0, len(outs) // n * DV)
    total = dot(hidden, mine[:, columns]) + dot(other, theirs[:, columns])
    for i, out in enumerate(outs):
        rows, columns = (i % n) * HALF, (i // n) * DV
        out[...] = total[rows: rows + HALF, columns: columns + DV].astype(out.dtype)


def partial(hidden, other, mine, theirs, kinds, name, after=()):
    n = len(hidden)
    width = len(kinds) // n * DV
    return call(
        functools.partial(partial_body, n),
        [((HALF, DV), kind) for kind in kinds],
        [VM] * (2 * n + 2),
        [*hidden, *other, mine, theirs],
        name,
        flops=4 * n * HALF * DV * width,
        moved=4 * DV * width,
        after=after,
    )


def mine_body(h0, h1, weight, out):
    for i, h in enumerate((h0, h1)):
        out[i * HALF: (i + 1) * HALF, :] = dot(h[...], weight[...])


def far_body(half, mine, other, weight, out):
    out[...] = (mine[pl.ds(half * HALF, HALF), :] + dot(other[...], weight[...])).astype(BF)


def own_body(h0, h1, o0, o1, mine, theirs, top, low, out_top, out_low):
    columns = pl.ds(2 * DV, DV)
    for h, o, come, out in ((h0, o0, top, out_top), (h1, o1, low, out_low)):
        out[...] = dot(h[...], mine[:, columns]) + dot(o[...], theirs[:, columns]) + come[...].astype(F32)


def final_body(own_top, own_low, top, low, out):
    out[:HALF, :] = (own_top[...] + top[...].astype(F32)).astype(BF)
    out[HALF:, :] = (own_low[...] + low[...].astype(F32)).astype(BF)


def added(mine, come):
    return (mine + come.astype(F32)).astype(BF)


def shards(tokens, w_query, w_key, w_value, w_gate, w_out, log_decay):
    w_out = pltpu.with_memory_space_constraint(w_out, pltpu.HBM)

    top, low = call(
        cut_body, [((HALF, WIDE), BF)] * 2, [ANY], [tokens], "cut", scratch=[pltpu.SemaphoreType.DMA((2,))],
        moved=ROWS * WIDE * 4,
    )
    a1, a3 = y_flip(top, 1), y_flip(low, 3)
    b1, b3 = y_flip(low, 1), y_flip(top, 3)
    own_s = tp_swap(tokens)
    remain, decay, factor, mask = call(
        decay_body,
        [((ROWS, 1), F32)] * 2 + [((1, DV), F32), ((ROWS, ROWS), F32)],
        [VM],
        [log_decay],
        "decay",
    )
    given_far, given, kept_far, kept = call(
        pick_body, [((DV, DV), BF), ((DV, 3 * DV), BF)] * 2, [HBM], [w_out], "pick",
        scratch=[pltpu.SemaphoreType.DMA((SIDE, 2))], moved=1,
    )
    kv = (w_key, w_value)
    sums = project(((0, 1), (0, 0)), (tokens, own_s), kv, None, "kv_own", hint=0)
    a1, a3 = tie((a1, a3), [kept_far, mask, sums[0]], "tie_a")
    c3, c1 = y_flip(a1, 3), y_flip(a3, 1)
    theirs_far, theirs = tp_swap(given_far), tp_swap(given)

    near1, near3 = call(join_body, [((ROWS, WIDE), BF)] * 2, [VM] * 4, [a1, b1, b3, a3], "join", moved=1)
    near1_s, near3_s = tp_swap(near1), tp_swap(near3)
    sums = project(((1, 1), (3, 1)), (near1, near3), kv, sums, "kv_near", hint=0)
    across = tie((c3, c1), sums[:1], "tie_c")
    across_s = tuple(tp_swap(p) for p in across)
    sums = project(((2, 1),), (tuple(across),), kv, sums, "kv_far", hint=10)
    sums = project(((1, 0), (3, 0)), (near1_s, near3_s), kv, sums, "kv_near_s", hint=0)
    keys, values, mine, m1, m2, m3 = call(
        state_body,
        [((ROWS, DK), BF), ((ROWS, DV), BF), ((CUT, DV), F32)] + [((MSG, DV), BF)] * 3,
        [VM] * 8,
        [*across_s, *sums, w_key, w_value, remain, factor],
        "state",
        scratch=[pltpu.VMEM((DK, DV), F32)],
        flops=2 * ROWS * (WIDE * (DK + DV) + DK * DV),
        moved=WIDE * (DK + DV) * 2,
    )
    messages = [z_flip(m, k + 1) for k, m in enumerate((m1, m2, m3))]

    everything = (tokens, own_s, near1, near3, near1_s, near3_s, tuple(across), across_s)
    order = ((0, 1), (0, 0), (1, 1), (3, 1), (1, 0), (3, 0), (2, 1), (2, 0))
    (query_sum,) = project(order, everything, (w_query,), None, "queries", after=[keys])
    (line,) = call(
        line_body, [((MSG, DV), BF)], [VM] * 5, [mine, factor, *messages], "line", moved=MSG * DV * 8,
        after=[query_sum],
    )
    lines = [x_flip(line, k) for k in range(1, SIDE)]
    (gates,) = project(order, everything, (w_gate,), None, "gates", after=[line], gated=True)
    e0, e1, e2, e3 = call(
        entry_body, [((CUT, DV), BF)] * 4, [VM] * 8, [mine, factor, *messages, *lines], "entry",
        moved=MSG * DV * 16, after=[gates],
    )
    queries, local = call(
        local_body,
        [((ROWS, DK), BF), ((ROWS, DV), F32)],
        [VM] * 4,
        [query_sum, keys, values, mask],
        "local",
        flops=2 * ROWS * ROWS * (DK + DV),
        moved=ROWS * DV * 4,
        after=[e0],
    )
    e1, e2, e3 = (z_flip(e, k + 1) for k, e in enumerate((e1, e2, e3)))
    hidden, other, far = [], [], []
    for half in range(2):
        (part,) = call(
            functools.partial(hidden_body, half), [((HALF, DV), BF)], [VM] * 8,
            [queries, e0, e1, e2, e3, local, decay, gates], f"hidden{half}",
            scratch=[pltpu.VMEM((DK, DV), BF)], flops=ROWS * DK * DV, moved=ROWS * DV * 4, after=hidden,
        )
        hidden.append(part)
        other.append(tp_swap(part))
    (mine,) = call(
        mine_body, [((ROWS, DV), F32)], [VM] * 3, [*hidden, kept_far], "far_mine", flops=2 * ROWS * DV * DV, moved=2 * DV * DV
    )
    for half in range(2):
        far += call(
            functools.partial(far_body, half), [((HALF, DV), BF)], [VM] * 3, [mine, other[half], theirs_far], f"far{half}",
            flops=2 * HALF * DV * DV, moved=2 * DV * DV, after=far,
        )
    via3, via1 = y_flip(far[0], 3), y_flip(far[1], 1)
    top1, low1, top3, low3 = partial(hidden, other, kept, theirs, (F32, BF, BF, F32), "beside", after=far)
    from1_low, from3_top = y_flip(low1, 1), y_flip(top3, 3)
    from1_top, from3_low = y_flip(added(top1, via3), 1), y_flip(added(low3, via1), 3)
    own = call(
        own_body, [((HALF, DV), F32)] * 2, [VM] * 8, [*hidden, *other, kept, theirs, from3_top, from1_low], "own",
        flops=4 * ROWS * DV * DV, moved=8 * DV * DV,
    )
    (out,) = call(
        final_body, [((ROWS, DV), BF)], [VM] * 4, [*own, from1_top, from3_low], "final", moved=ROWS * DV * 2,
    )
    return out


def solution(mesh):
    in_specs = (P("ctx", "tp"),) + (P(None, "tp"),) * 4 + (P("tp", None), P("tp", "ctx"))
    return jax.shard_map(
        shards, mesh=mesh, in_specs=in_specs, out_specs=P("ctx", "tp"), check_vma=False
    )
```

```python
import functools

import jax
import jax.numpy as jnp
from jax import lax
from jax.experimental import pallas as pl
from jax.experimental.pallas import tpu as pltpu
from jax.sharding import PartitionSpec as P

DK = 256
DV = 512
ROWS = 512
HALF = 256
WIDE = 512
SIDE = 4
CUT = DK // SIDE
MSG = CUT + 16
BF, F32 = jnp.bfloat16, jnp.float32
VM = pl.BlockSpec(memory_space=pltpu.VMEM)
ANY = pl.BlockSpec(memory_space=pl.ANY)
HBM = pl.BlockSpec(memory_space=pltpu.HBM)


def turn(k, core):
    return k ^ (2 * (1 - core)) if k % 2 else k


def meet(k, core, order):
    return turn(order[k], core)


Z_ORDER, X_ORDER = (0, 2, 1, 3), (0, 2, 1, 3)


def y_flip(value, k):
    return lax.ppermute(value, "tp", [(i, i ^ (2 * turn(k, i % 2))) for i in range(8)])


def tp_swap(value):
    return lax.ppermute(value, "tp", [(i, i ^ 1) for i in range(8)])


def z_flip(value, k):
    return ctx_flip(value, k, 1)


def x_flip(value, k):
    return ctx_flip(value, k, 4)


def ctx_flip(value, k, unit):
    pairs = [(8 * i + j, 8 * (i ^ (unit * meet(k, j % 2, Z_ORDER if unit == 1 else X_ORDER))) + j) for i in range(16) for j in range(8)]
    return lax.ppermute(value, ("ctx", "tp"), pairs)


def my(name):
    ctx, tp = lax.axis_index("ctx"), lax.axis_index("tp")
    return {"x": ctx // SIDE, "z": ctx % SIDE, "y": tp // 2, "core": tp % 2}[name]


def rows_of(step, same):
    core = my("core") if same else 1 - my("core")
    return pl.ds(pl.multiple_of((2 * (my("y") ^ turn(step, core)) + core) * WIDE, WIDE), WIDE)


def dot(a, b):
    return jnp.dot(a, b, preferred_element_type=F32)


def call(body, outs, in_specs, args, name, scratch=(), flops=0, moved=0, limit=16, out_specs=None, after=()):
    shapes = [jax.ShapeDtypeStruct(shape, dtype) for shape, dtype in outs]

    def whole(*refs):
        body(*refs[: len(args)], *refs[len(args) + len(after):])

    return pl.pallas_call(
        whole,
        out_shape=shapes,
        in_specs=list(in_specs) + [ANY] * len(after),
        out_specs=out_specs or [VM] * len(shapes),
        scratch_shapes=list(scratch),
        name=name,
        cost_estimate=pl.CostEstimate(flops=flops, bytes_accessed=moved, transcendentals=0),
        compiler_params=pltpu.CompilerParams(vmem_limit_bytes=limit * 1024 * 1024),
    )(*args, *after)


def join_body(top1, low1, top3, low3, near1, near3):
    for top, low, near in ((top1, low1, near1), (top3, low3, near3)):
        near[:HALF, :] = top[...]
        near[HALF:, :] = low[...]


def project_body(owners, halves, n_weights, started, gated, *refs):
    shards = []
    for half in halves:
        if half:
            shards.append(jnp.concatenate([refs[0][...], refs[1][...]], axis=0))
        else:
            shards.append(refs[0][...])
        refs = refs[2 if half else 1:]
    weights, refs = refs[:n_weights], refs[n_weights:]
    sums, outs = (refs[:n_weights], refs[n_weights:]) if started else ([None] * n_weights, refs)
    for weight, before, out in zip(weights, sums, outs):
        total = None if before is None else before[...]
        for shard, owner in zip(shards, owners):
            new = dot(shard, weight[rows_of(*owner), :])
            total = new if total is None else total + new
        out[...] = gate_of(total) if gated else total


def gate_of(total):
    gate = total.astype(BF).astype(F32)
    return gate / (1.0 + jnp.exp(-gate))


def project(owners, shards, weights, before, name, after=(), gated=False, hint=1):
    halves = [isinstance(s, tuple) for s in shards]
    flat = [p for s in shards for p in (s if isinstance(s, tuple) else (s,))]
    n = len(weights)
    widths = [w.shape[1] for w in weights]
    return call(
        functools.partial(project_body, owners, halves, n, before is not None, gated),
        [((ROWS, width), F32) for width in widths],
        [VM] * (len(flat) + n + (n if before else 0)),
        [*flat, *weights, *(before or [])],
        name,
        flops=2 * ROWS * WIDE * len(owners) * sum(widths) * hint + 1,
        moved=WIDE * len(owners) * sum(widths) * 2 * hint + 1,
        after=after,
    )


def tie(values, after, name):
    n = len(values)

    def body(*refs):
        pass

    return pl.pallas_call(
        body,
        out_shape=[jax.ShapeDtypeStruct(v.shape, v.dtype) for v in values],
        in_specs=[ANY] * (n + len(after)),
        out_specs=[ANY] * n,
        input_output_aliases={i: i for i in range(n)},
        name=name,
        compiler_params=pltpu.CompilerParams(vmem_limit_bytes=4 * 1024 * 1024),
    )(*values, *after)


def state_body(own0, own1, key_sum, value_sum, wk, wv, remain, factor, keys, values, mine, m1, m2, m3, state):
    x = jnp.concatenate([own0[...], own1[...]], axis=0)
    rows = rows_of(2, 0)
    k = ((key_sum[...] + dot(x, wk[rows, :])) * DK ** (-0.5)).astype(BF)
    v = (value_sum[...] + dot(x, wv[rows, :])).astype(BF)
    keys[...] = k
    values[...] = v
    weighted = (k.astype(F32) * remain[...]).astype(BF)
    state[...] = lax.dot_general(weighted, v, (((0,), (0,)), ((), ())), preferred_element_type=F32)
    z = my("z")
    total = factor[...]
    high = total.astype(BF)
    rest = (total - high.astype(F32)).astype(BF)
    for i, ref in enumerate((mine, m1, m2, m3)):
        piece = state[pl.ds(pl.multiple_of((z ^ meet(i, my("core"), Z_ORDER)) * CUT, CUT), CUT), :]
        if i == 0:
            ref[...] = piece
        else:
            ref[...] = jnp.concatenate(
                [piece.astype(BF), jnp.broadcast_to(high, (8, DV)), jnp.broadcast_to(rest, (8, DV))], axis=0
            )


def open_message(ref):
    ends = ref[CUT:, :].astype(F32)
    return ref[:CUT, :].astype(F32), ends[0:1] + ends[8:9]


def between(factors, sources, low, high):
    product = jnp.ones_like(factors[0])
    for factor, source in zip(factors, sources):
        product = product * jnp.where((source > low) & (source < high), factor, 1.0)
    return product


def prefix(pieces, factors, sources, target):
    total = jnp.zeros_like(pieces[0])
    for piece, source in zip(pieces, sources):
        weight = between(factors, sources, source, target)
        total = total + jnp.where(source < target, weight, 0.0) * piece
    return total


def line_of(mine, factor, messages):
    opened = [open_message(m) for m in messages]
    z = my("z")
    pieces = [mine[...]] + [piece for piece, _ in opened]
    factors = [factor[...]] + [f for _, f in opened]
    return pieces, factors, [z ^ meet(k, my("core"), Z_ORDER) for k in range(SIDE)]


def line_body(mine, factor, m1, m2, m3, out):
    pieces, factors, sources = line_of(mine, factor, (m1, m2, m3))
    total = between(factors, sources, -1, SIDE)
    high = total.astype(BF)
    rest = (total - high.astype(F32)).astype(BF)
    piece = prefix(pieces, factors, sources, SIDE)
    out[...] = jnp.concatenate(
        [piece.astype(BF), jnp.broadcast_to(high, (8, DV)), jnp.broadcast_to(rest, (8, DV))], axis=0
    )


def entry_body(mine, factor, m1, m2, m3, n1, n2, n3, e0, e1, e2, e3):
    pieces, factors, sources = line_of(mine, factor, (m1, m2, m3))
    x, z = my("x"), my("z")
    opened = [open_message(n) for n in (n1, n2, n3)]
    entry = prefix([p for p, _ in opened], [f for _, f in opened], [x ^ meet(k, my("core"), X_ORDER) for k in range(1, SIDE)], x)
    for k, ref in enumerate((e0, e1, e2, e3)):
        target = z ^ meet(k, my("core"), Z_ORDER)
        whole = prefix(pieces, factors, sources, target) + between(factors, sources, -1, target) * entry
        ref[...] = whole.astype(BF)


def decay_body(rates, remain, decay, factor, mask):
    rows = lax.broadcasted_iota(jnp.int32, (ROWS, ROWS), 0)
    cols = lax.broadcasted_iota(jnp.int32, (ROWS, ROWS), 1)
    rate_row = jnp.broadcast_to(rates[...], (ROWS, ROWS))
    rate_col = jnp.sum(jnp.where(rows == cols, rate_row, 0.0), axis=1, keepdims=True)
    cumul_col = jnp.sum(jnp.where(rows >= cols, rate_row, 0.0), axis=1, keepdims=True)
    cumul_row = jnp.sum(jnp.where(rows <= cols, rate_col, 0.0), axis=0, keepdims=True)
    total = cumul_col[ROWS - 1:]
    remain[...] = jnp.exp(total - cumul_col)
    decay[...] = jnp.exp(cumul_col)
    factor[...] = jnp.broadcast_to(jnp.exp(total), (1, DV))
    mask[...] = jnp.exp(jnp.where(rows >= cols, cumul_col - cumul_row, -1e30))


def local_body(query_sum, keys, values, mask, queries, local):
    q = query_sum[...].astype(BF)
    queries[...] = q
    scores = lax.dot_general(q, keys[...], (((1,), (1,)), ((), ())), preferred_element_type=F32)
    local[...] = dot((scores * mask[...]).astype(BF), values[...])


def hidden_body(half, queries, e0, e1, e2, e3, local, decay, gates, hidden, whole):
    z = my("z")
    rows = pl.ds(half * HALF, HALF)
    for k, ref in enumerate((e0, e1, e2, e3)):
        whole[pl.ds(pl.multiple_of((z ^ meet(k, my("core"), Z_ORDER)) * CUT, CUT), CUT), :] = ref[...]
    retained = local[rows, :] + decay[rows, :] * dot(queries[rows, :], whole[...])
    center = retained - jnp.mean(retained, axis=-1, keepdims=True)
    variance = jnp.mean(center * center, axis=-1, keepdims=True)
    hidden[...] = (gates[rows, :] * (center * lax.rsqrt(variance + 1e-5))).astype(BF)


def cut_body(tokens, top, low, sems):
    copies = [
        pltpu.make_async_copy(tokens.at[pl.ds(i * HALF, HALF), :], out, sems.at[i]) for i, out in enumerate((top, low))
    ]
    for copy in copies:
        copy.start()
    for copy in copies:
        copy.wait()


STEPS = (2, 1, 3, 0)


def pick_body(weight, given_far, given, kept_far, kept, sems):
    core, y = my("core"), my("y")
    copies = []
    for i, step in enumerate(STEPS):
        for j, (outs, which) in enumerate((((given_far, given), 1 - core), ((kept_far, kept), core))):
            block = y ^ turn(step, which)
            columns = pl.ds(pl.multiple_of((2 * block + which) * DV, DV), DV)
            out = outs[0] if i == 0 else outs[1].at[:, pl.ds((i - 1) * DV, DV)]
            copy = pltpu.make_async_copy(weight.at[:, columns], out, sems.at[i, j])
            copy.start()
            copies.append(copy)
    for copy in copies:
        copy.wait()


def partial_body(n, *refs):
    hidden = jnp.concatenate([r[...] for r in refs[:n]], axis=0)
    other = jnp.concatenate([r[...] for r in refs[n: 2 * n]], axis=0)
    mine, theirs, outs = refs[2 * n], refs[2 * n + 1], refs[2 * n + 2:]
    columns = pl.ds(0, len(outs) // n * DV)
    total = dot(hidden, mine[:, columns]) + dot(other, theirs[:, columns])
    for i, out in enumerate(outs):
        rows, columns = (i % n) * HALF, (i // n) * DV
        out[...] = total[rows: rows + HALF, columns: columns + DV].astype(out.dtype)


def partial(hidden, other, mine, theirs, kinds, name, after=()):
    n = len(hidden)
    width = len(kinds) // n * DV
    return call(
        functools.partial(partial_body, n),
        [((HALF, DV), kind) for kind in kinds],
        [VM] * (2 * n + 2),
        [*hidden, *other, mine, theirs],
        name,
        flops=4 * n * HALF * DV * width,
        moved=4 * DV * width,
        after=after,
    )


def far_body(h0, h1, o0, o1, mine, theirs, top, low):
    for h, o, out in ((h0, o0, top), (h1, o1, low)):
        out[...] = (dot(h[...], mine[...]) + dot(o[...], theirs[...])).astype(BF)


def own_body(h0, h1, o0, o1, mine, theirs, top, low, out_top, out_low):
    columns = pl.ds(2 * DV, DV)
    for h, o, come, out in ((h0, o0, top, out_top), (h1, o1, low, out_low)):
        out[...] = dot(h[...], mine[:, columns]) + dot(o[...], theirs[:, columns]) + come[...].astype(F32)


def final_body(own_top, own_low, top, low, out):
    out[:HALF, :] = (own_top[...] + top[...].astype(F32)).astype(BF)
    out[HALF:, :] = (own_low[...] + low[...].astype(F32)).astype(BF)


def added(mine, come):
    return (mine + come.astype(F32)).astype(BF)


def shards(tokens, w_query, w_key, w_value, w_gate, w_out, log_decay):
    w_out = pltpu.with_memory_space_constraint(w_out, pltpu.HBM)

    top, low = call(
        cut_body, [((HALF, WIDE), BF)] * 2, [ANY], [tokens], "cut", scratch=[pltpu.SemaphoreType.DMA((2,))],
        moved=ROWS * WIDE * 4,
    )
    a1, a3 = y_flip(top, 1), y_flip(low, 3)
    b1, b3 = y_flip(low, 1), y_flip(top, 3)
    own_s = tp_swap(tokens)
    remain, decay, factor, mask = call(
        decay_body,
        [((ROWS, 1), F32)] * 2 + [((1, DV), F32), ((ROWS, ROWS), F32)],
        [VM],
        [log_decay],
        "decay",
    )
    given_far, given, kept_far, kept = call(
        pick_body, [((DV, DV), BF), ((DV, 3 * DV), BF)] * 2, [HBM], [w_out], "pick",
        scratch=[pltpu.SemaphoreType.DMA((SIDE, 2))], moved=1,
    )
    kv = (w_key, w_value)
    sums = project(((0, 1), (0, 0)), (tokens, own_s), kv, None, "kv_own", hint=0)
    a1, a3 = tie((a1, a3), [kept_far, mask, sums[0]], "tie_a")
    c3, c1 = y_flip(a1, 3), y_flip(a3, 1)
    theirs_far, theirs = tp_swap(given_far), tp_swap(given)

    near1, near3 = call(join_body, [((ROWS, WIDE), BF)] * 2, [VM] * 4, [a1, b1, b3, a3], "join", moved=1)
    near1_s, near3_s = tp_swap(near1), tp_swap(near3)
    sums = project(((1, 1), (3, 1)), (near1, near3), kv, sums, "kv_near", hint=0)
    across = tie((c3, c1), sums[:1], "tie_c")
    across_s = tuple(tp_swap(p) for p in across)
    sums = project(((2, 1),), (tuple(across),), kv, sums, "kv_far", hint=10)
    sums = project(((1, 0), (3, 0)), (near1_s, near3_s), kv, sums, "kv_near_s", hint=0)
    keys, values, mine, m1, m2, m3 = call(
        state_body,
        [((ROWS, DK), BF), ((ROWS, DV), BF), ((CUT, DV), F32)] + [((MSG, DV), BF)] * 3,
        [VM] * 8,
        [*across_s, *sums, w_key, w_value, remain, factor],
        "state",
        scratch=[pltpu.VMEM((DK, DV), F32)],
        flops=2 * ROWS * (WIDE * (DK + DV) + DK * DV),
        moved=WIDE * (DK + DV) * 2,
    )
    messages = [z_flip(m, k + 1) for k, m in enumerate((m1, m2, m3))]

    everything = (tokens, own_s, near1, near3, near1_s, near3_s, tuple(across), across_s)
    order = ((0, 1), (0, 0), (1, 1), (3, 1), (1, 0), (3, 0), (2, 1), (2, 0))
    (gates,) = project(order, everything, (w_gate,), None, "gates", after=[keys], gated=True)
    (line,) = call(
        line_body, [((MSG, DV), BF)], [VM] * 5, [mine, factor, *messages], "line", moved=MSG * DV * 8,
        after=[gates],
    )
    lines = [x_flip(line, k) for k in range(1, SIDE)]
    (query_sum,) = project(order, everything, (w_query,), None, "queries", after=[line])
    e0, e1, e2, e3 = call(
        entry_body, [((CUT, DV), BF)] * 4, [VM] * 8, [mine, factor, *messages, *lines], "entry",
        moved=MSG * DV * 16, after=[query_sum],
    )
    queries, local = call(
        local_body,
        [((ROWS, DK), BF), ((ROWS, DV), F32)],
        [VM] * 4,
        [query_sum, keys, values, mask],
        "local",
        flops=2 * ROWS * ROWS * (DK + DV),
        moved=ROWS * DV * 4,
        after=[e0],
    )
    e1, e2, e3 = (z_flip(e, k + 1) for k, e in enumerate((e1, e2, e3)))
    hidden, other, far = [], [], []
    for half in range(2):
        (part,) = call(
            functools.partial(hidden_body, half), [((HALF, DV), BF)], [VM] * 8,
            [queries, e0, e1, e2, e3, local, decay, gates], f"hidden{half}",
            scratch=[pltpu.VMEM((DK, DV), BF)], flops=ROWS * DK * DV, moved=ROWS * DV * 4, after=hidden,
        )
        hidden.append(part)
        other.append(tp_swap(part))
    far = call(
        far_body, [((HALF, DV), BF)] * 2, [VM] * 6, [*hidden, *other, kept_far, theirs_far], "far",
        flops=4 * ROWS * DV * DV, moved=4 * DV * DV,
    )
    via3, via1 = y_flip(far[0], 3), y_flip(far[1], 1)
    top1, low1, top3, low3 = partial(hidden, other, kept, theirs, (F32, BF, BF, F32), "beside", after=far)
    from1_low, from3_top = y_flip(low1, 1), y_flip(top3, 3)
    from1_top, from3_low = y_flip(added(top1, via3), 1), y_flip(added(low3, via1), 3)
    own = call(
        own_body, [((HALF, DV), F32)] * 2, [VM] * 8, [*hidden, *other, kept, theirs, from3_top, from1_low], "own",
        flops=4 * ROWS * DV * DV, moved=8 * DV * DV,
    )
    (out,) = call(
        final_body, [((ROWS, DV), BF)], [VM] * 4, [*own, from1_top, from3_low], "final", moved=ROWS * DV * 2,
    )
    return out


def solution(mesh):
    in_specs = (P("ctx", "tp"),) + (P(None, "tp"),) * 4 + (P("tp", None), P("tp", "ctx"))
    return jax.shard_map(
        shards, mesh=mesh, in_specs=in_specs, out_specs=P("ctx", "tp"), check_vma=False
    )
```

```python
import functools

import jax
import jax.numpy as jnp
from jax import lax
from jax.experimental import pallas as pl
from jax.experimental.pallas import tpu as pltpu
from jax.sharding import PartitionSpec as P

DK = 256
DV = 512
ROWS = 512
HALF = 256
WIDE = 512
SIDE = 4
CUT = DK // SIDE
MSG = CUT + 16
BF, F32 = jnp.bfloat16, jnp.float32
VM = pl.BlockSpec(memory_space=pltpu.VMEM)
ANY = pl.BlockSpec(memory_space=pl.ANY)
HBM = pl.BlockSpec(memory_space=pltpu.HBM)


def turn(k, core):
    return k ^ (2 * (1 - core)) if k % 2 else k


def meet(k, core, order):
    return turn(order[k], core)


Z_ORDER, X_ORDER = (0, 2, 1, 3), (0, 2, 1, 3)


def y_flip(value, k):
    return lax.ppermute(value, "tp", [(i, i ^ (2 * turn(k, i % 2))) for i in range(8)])


def tp_swap(value):
    return lax.ppermute(value, "tp", [(i, i ^ 1) for i in range(8)])


def z_flip(value, k):
    return ctx_flip(value, k, 1)


def x_flip(value, k):
    return ctx_flip(value, k, 4)


def ctx_flip(value, k, unit):
    pairs = [(8 * i + j, 8 * (i ^ (unit * meet(k, j % 2, Z_ORDER if unit == 1 else X_ORDER))) + j) for i in range(16) for j in range(8)]
    return lax.ppermute(value, ("ctx", "tp"), pairs)


def my(name):
    ctx, tp = lax.axis_index("ctx"), lax.axis_index("tp")
    return {"x": ctx // SIDE, "z": ctx % SIDE, "y": tp // 2, "core": tp % 2}[name]


def rows_of(step, same):
    core = my("core") if same else 1 - my("core")
    return pl.ds(pl.multiple_of((2 * (my("y") ^ turn(step, core)) + core) * WIDE, WIDE), WIDE)


def dot(a, b):
    return jnp.dot(a, b, preferred_element_type=F32)


def call(body, outs, in_specs, args, name, scratch=(), flops=0, moved=0, limit=16, out_specs=None, after=()):
    shapes = [jax.ShapeDtypeStruct(shape, dtype) for shape, dtype in outs]

    def whole(*refs):
        body(*refs[: len(args)], *refs[len(args) + len(after):])

    return pl.pallas_call(
        whole,
        out_shape=shapes,
        in_specs=list(in_specs) + [ANY] * len(after),
        out_specs=out_specs or [VM] * len(shapes),
        scratch_shapes=list(scratch),
        name=name,
        cost_estimate=pl.CostEstimate(flops=flops, bytes_accessed=moved, transcendentals=0),
        compiler_params=pltpu.CompilerParams(vmem_limit_bytes=limit * 1024 * 1024),
    )(*args, *after)


def join_body(top1, low1, top3, low3, near1, near3):
    for top, low, near in ((top1, low1, near1), (top3, low3, near3)):
        near[:HALF, :] = top[...]
        near[HALF:, :] = low[...]


def project_body(owners, halves, n_weights, started, gated, *refs):
    shards = []
    for half in halves:
        if half:
            shards.append(jnp.concatenate([refs[0][...], refs[1][...]], axis=0))
        else:
            shards.append(refs[0][...])
        refs = refs[2 if half else 1:]
    weights, refs = refs[:n_weights], refs[n_weights:]
    sums, outs = (refs[:n_weights], refs[n_weights:]) if started else ([None] * n_weights, refs)
    for weight, before, out in zip(weights, sums, outs):
        total = None if before is None else before[...]
        for shard, owner in zip(shards, owners):
            new = dot(shard, weight[rows_of(*owner), :])
            total = new if total is None else total + new
        out[...] = gate_of(total) if gated else total


def gate_of(total):
    gate = total.astype(BF).astype(F32)
    return gate / (1.0 + jnp.exp(-gate))


def project(owners, shards, weights, before, name, after=(), gated=False, hint=1):
    halves = [isinstance(s, tuple) for s in shards]
    flat = [p for s in shards for p in (s if isinstance(s, tuple) else (s,))]
    n = len(weights)
    widths = [w.shape[1] for w in weights]
    return call(
        functools.partial(project_body, owners, halves, n, before is not None, gated),
        [((ROWS, width), F32) for width in widths],
        [VM] * (len(flat) + n + (n if before else 0)),
        [*flat, *weights, *(before or [])],
        name,
        flops=2 * ROWS * WIDE * len(owners) * sum(widths) * hint + 1,
        moved=WIDE * len(owners) * sum(widths) * 2 * hint + 1,
        after=after,
    )


def tie(values, after, name):
    n = len(values)

    def body(*refs):
        pass

    return pl.pallas_call(
        body,
        out_shape=[jax.ShapeDtypeStruct(v.shape, v.dtype) for v in values],
        in_specs=[ANY] * (n + len(after)),
        out_specs=[ANY] * n,
        input_output_aliases={i: i for i in range(n)},
        name=name,
        compiler_params=pltpu.CompilerParams(vmem_limit_bytes=4 * 1024 * 1024),
    )(*values, *after)


def state_body(own0, own1, key_sum, value_sum, wk, wv, remain, factor, keys, values, mine, m1, m2, m3, state):
    x = jnp.concatenate([own0[...], own1[...]], axis=0)
    rows = rows_of(2, 0)
    k = ((key_sum[...] + dot(x, wk[rows, :])) * DK ** (-0.5)).astype(BF)
    v = (value_sum[...] + dot(x, wv[rows, :])).astype(BF)
    keys[...] = k
    values[...] = v
    weighted = (k.astype(F32) * remain[...]).astype(BF)
    state[...] = lax.dot_general(weighted, v, (((0,), (0,)), ((), ())), preferred_element_type=F32)
    z = my("z")
    total = factor[...]
    high = total.astype(BF)
    rest = (total - high.astype(F32)).astype(BF)
    for i, ref in enumerate((mine, m1, m2, m3)):
        piece = state[pl.ds(pl.multiple_of((z ^ meet(i, my("core"), Z_ORDER)) * CUT, CUT), CUT), :]
        if i == 0:
            ref[...] = piece
        else:
            ref[...] = jnp.concatenate(
                [piece.astype(BF), jnp.broadcast_to(high, (8, DV)), jnp.broadcast_to(rest, (8, DV))], axis=0
            )


def open_message(ref):
    ends = ref[CUT:, :].astype(F32)
    return ref[:CUT, :].astype(F32), ends[0:1] + ends[8:9]


def between(factors, sources, low, high):
    product = jnp.ones_like(factors[0])
    for factor, source in zip(factors, sources):
        product = product * jnp.where((source > low) & (source < high), factor, 1.0)
    return product


def prefix(pieces, factors, sources, target):
    total = jnp.zeros_like(pieces[0])
    for piece, source in zip(pieces, sources):
        weight = between(factors, sources, source, target)
        total = total + jnp.where(source < target, weight, 0.0) * piece
    return total


def line_of(mine, factor, messages):
    opened = [open_message(m) for m in messages]
    z = my("z")
    pieces = [mine[...]] + [piece for piece, _ in opened]
    factors = [factor[...]] + [f for _, f in opened]
    return pieces, factors, [z ^ meet(k, my("core"), Z_ORDER) for k in range(SIDE)]


def line_body(mine, factor, m1, m2, m3, out):
    pieces, factors, sources = line_of(mine, factor, (m1, m2, m3))
    total = between(factors, sources, -1, SIDE)
    high = total.astype(BF)
    rest = (total - high.astype(F32)).astype(BF)
    piece = prefix(pieces, factors, sources, SIDE)
    out[...] = jnp.concatenate(
        [piece.astype(BF), jnp.broadcast_to(high, (8, DV)), jnp.broadcast_to(rest, (8, DV))], axis=0
    )


def entry_body(mine, factor, m1, m2, m3, n1, n2, n3, e0, e1, e2, e3):
    pieces, factors, sources = line_of(mine, factor, (m1, m2, m3))
    x, z = my("x"), my("z")
    opened = [open_message(n) for n in (n1, n2, n3)]
    entry = prefix([p for p, _ in opened], [f for _, f in opened], [x ^ meet(k, my("core"), X_ORDER) for k in range(1, SIDE)], x)
    for k, ref in enumerate((e0, e1, e2, e3)):
        target = z ^ meet(k, my("core"), Z_ORDER)
        whole = prefix(pieces, factors, sources, target) + between(factors, sources, -1, target) * entry
        ref[...] = whole.astype(BF)


def decay_body(rates, remain, decay, factor, mask):
    rows = lax.broadcasted_iota(jnp.int32, (ROWS, ROWS), 0)
    cols = lax.broadcasted_iota(jnp.int32, (ROWS, ROWS), 1)
    rate_row = jnp.broadcast_to(rates[...], (ROWS, ROWS))
    rate_col = jnp.sum(jnp.where(rows == cols, rate_row, 0.0), axis=1, keepdims=True)
    cumul_col = jnp.sum(jnp.where(rows >= cols, rate_row, 0.0), axis=1, keepdims=True)
    cumul_row = jnp.sum(jnp.where(rows <= cols, rate_col, 0.0), axis=0, keepdims=True)
    total = cumul_col[ROWS - 1:]
    remain[...] = jnp.exp(total - cumul_col)
    decay[...] = jnp.exp(cumul_col)
    factor[...] = jnp.broadcast_to(jnp.exp(total), (1, DV))
    mask[...] = jnp.exp(jnp.where(rows >= cols, cumul_col - cumul_row, -1e30))


def local_body(query_sum, keys, values, mask, queries, local):
    q = query_sum[...].astype(BF)
    queries[...] = q
    scores = lax.dot_general(q, keys[...], (((1,), (1,)), ((), ())), preferred_element_type=F32)
    local[...] = dot((scores * mask[...]).astype(BF), values[...])


def hidden_body(half, queries, e0, e1, e2, e3, local, decay, gates, hidden, whole):
    z = my("z")
    rows = pl.ds(half * HALF, HALF)
    for k, ref in enumerate((e0, e1, e2, e3)):
        whole[pl.ds(pl.multiple_of((z ^ meet(k, my("core"), Z_ORDER)) * CUT, CUT), CUT), :] = ref[...]
    retained = local[rows, :] + decay[rows, :] * dot(queries[rows, :], whole[...])
    center = retained - jnp.mean(retained, axis=-1, keepdims=True)
    variance = jnp.mean(center * center, axis=-1, keepdims=True)
    hidden[...] = (gates[rows, :] * (center * lax.rsqrt(variance + 1e-5))).astype(BF)


def cut_body(tokens, top, low, sems):
    copies = [
        pltpu.make_async_copy(tokens.at[pl.ds(i * HALF, HALF), :], out, sems.at[i]) for i, out in enumerate((top, low))
    ]
    for copy in copies:
        copy.start()
    for copy in copies:
        copy.wait()


STEPS = (2, 1, 3, 0)


def pick_body(weight, given_far, given, kept_far, kept, sems):
    core, y = my("core"), my("y")
    copies = []
    for i, step in enumerate(STEPS):
        for j, (outs, which) in enumerate((((given_far, given), 1 - core), ((kept_far, kept), core))):
            block = y ^ turn(step, which)
            columns = pl.ds(pl.multiple_of((2 * block + which) * DV, DV), DV)
            out = outs[0] if i == 0 else outs[1].at[:, pl.ds((i - 1) * DV, DV)]
            copy = pltpu.make_async_copy(weight.at[:, columns], out, sems.at[i, j])
            copy.start()
            copies.append(copy)
    for copy in copies:
        copy.wait()


def partial_body(n, *refs):
    hidden = jnp.concatenate([r[...] for r in refs[:n]], axis=0)
    other = jnp.concatenate([r[...] for r in refs[n: 2 * n]], axis=0)
    mine, theirs, outs = refs[2 * n], refs[2 * n + 1], refs[2 * n + 2:]
    columns = pl.ds(0, len(outs) // n * DV)
    total = dot(hidden, mine[:, columns]) + dot(other, theirs[:, columns])
    for i, out in enumerate(outs):
        rows, columns = (i % n) * HALF, (i // n) * DV
        out[...] = total[rows: rows + HALF, columns: columns + DV].astype(out.dtype)


def partial(hidden, other, mine, theirs, kinds, name, after=()):
    n = len(hidden)
    width = len(kinds) // n * DV
    return call(
        functools.partial(partial_body, n),
        [((HALF, DV), kind) for kind in kinds],
        [VM] * (2 * n + 2),
        [*hidden, *other, mine, theirs],
        name,
        flops=4 * n * HALF * DV * width,
        moved=4 * DV * width,
        after=after,
    )


def mine_body(h0, h1, weight, out):
    for i, h in enumerate((h0, h1)):
        out[i * HALF: (i + 1) * HALF, :] = dot(h[...], weight[...])


def far_body(half, mine, other, weight, out):
    out[...] = (mine[pl.ds(half * HALF, HALF), :] + dot(other[...], weight[...])).astype(BF)


def own_body(h0, h1, o0, o1, mine, theirs, top, low, out_top, out_low):
    columns = pl.ds(2 * DV, DV)
    for h, o, come, out in ((h0, o0, top, out_top), (h1, o1, low, out_low)):
        out[...] = dot(h[...], mine[:, columns]) + dot(o[...], theirs[:, columns]) + come[...].astype(F32)


def final_body(own_top, own_low, top, low, out):
    out[:HALF, :] = (own_top[...] + top[...].astype(F32)).astype(BF)
    out[HALF:, :] = (own_low[...] + low[...].astype(F32)).astype(BF)


def added(mine, come):
    return (mine + come.astype(F32)).astype(BF)


def shards(tokens, w_query, w_key, w_value, w_gate, w_out, log_decay):
    w_out = pltpu.with_memory_space_constraint(w_out, pltpu.HBM)

    top, low = call(
        cut_body, [((HALF, WIDE), BF)] * 2, [ANY], [tokens], "cut", scratch=[pltpu.SemaphoreType.DMA((2,))],
        moved=ROWS * WIDE * 4,
    )
    a1, a3 = y_flip(top, 1), y_flip(low, 3)
    b1, b3 = y_flip(low, 1), y_flip(top, 3)
    own_s = tp_swap(tokens)
    remain, decay, factor, mask = call(
        decay_body,
        [((ROWS, 1), F32)] * 2 + [((1, DV), F32), ((ROWS, ROWS), F32)],
        [VM],
        [log_decay],
        "decay",
    )
    given_far, given, kept_far, kept = call(
        pick_body, [((DV, DV), BF), ((DV, 3 * DV), BF)] * 2, [HBM], [w_out], "pick",
        scratch=[pltpu.SemaphoreType.DMA((SIDE, 2))], moved=1,
    )
    kv = (w_key, w_value)
    sums = project(((0, 1), (0, 0)), (tokens, own_s), kv, None, "kv_own", hint=0)
    a1, a3 = tie((a1, a3), [kept_far, mask, sums[0]], "tie_a")
    c3, c1 = y_flip(a1, 3), y_flip(a3, 1)
    theirs_far, theirs = tp_swap(given_far), tp_swap(given)

    near1, near3 = call(join_body, [((ROWS, WIDE), BF)] * 2, [VM] * 4, [a1, b1, b3, a3], "join", moved=1)
    near1_s, near3_s = tp_swap(near1), tp_swap(near3)
    sums = project(((1, 1), (3, 1)), (near1, near3), kv, sums, "kv_near", hint=0)
    across = tie((c3, c1), sums[:1], "tie_c")
    across_s = tuple(tp_swap(p) for p in across)
    sums = project(((2, 1),), (tuple(across),), kv, sums, "kv_far", hint=10)
    sums = project(((1, 0), (3, 0)), (near1_s, near3_s), kv, sums, "kv_near_s", hint=0)
    keys, values, mine, m1, m2, m3 = call(
        state_body,
        [((ROWS, DK), BF), ((ROWS, DV), BF), ((CUT, DV), F32)] + [((MSG, DV), BF)] * 3,
        [VM] * 8,
        [*across_s, *sums, w_key, w_value, remain, factor],
        "state",
        scratch=[pltpu.VMEM((DK, DV), F32)],
        flops=2 * ROWS * (WIDE * (DK + DV) + DK * DV),
        moved=WIDE * (DK + DV) * 2,
    )
    messages = [z_flip(m, k + 1) for k, m in enumerate((m1, m2, m3))]

    everything = (tokens, own_s, near1, near3, near1_s, near3_s, tuple(across), across_s)
    order = ((0, 1), (0, 0), (1, 1), (3, 1), (1, 0), (3, 0), (2, 1), (2, 0))
    (gates,) = project(order, everything, (w_gate,), None, "gates", after=[keys], gated=True)
    (line,) = call(
        line_body, [((MSG, DV), BF)], [VM] * 5, [mine, factor, *messages], "line", moved=MSG * DV * 8,
        after=[gates],
    )
    lines = [x_flip(line, k) for k in range(1, SIDE)]
    (query_sum,) = project(order, everything, (w_query,), None, "queries", after=[line])
    e0, e1, e2, e3 = call(
        entry_body, [((CUT, DV), BF)] * 4, [VM] * 8, [mine, factor, *messages, *lines], "entry",
        moved=MSG * DV * 16, after=[query_sum],
    )
    queries, local = call(
        local_body,
        [((ROWS, DK), BF), ((ROWS, DV), F32)],
        [VM] * 4,
        [query_sum, keys, values, mask],
        "local",
        flops=2 * ROWS * ROWS * (DK + DV),
        moved=ROWS * DV * 4,
        after=[e0],
    )
    e1, e2, e3 = (z_flip(e, k + 1) for k, e in enumerate((e1, e2, e3)))
    hidden, other, far = [], [], []
    for half in range(2):
        (part,) = call(
            functools.partial(hidden_body, half), [((HALF, DV), BF)], [VM] * 8,
            [queries, e0, e1, e2, e3, local, decay, gates], f"hidden{half}",
            scratch=[pltpu.VMEM((DK, DV), BF)], flops=ROWS * DK * DV, moved=ROWS * DV * 4, after=hidden,
        )
        hidden.append(part)
        other.append(tp_swap(part))
    (mine,) = call(
        mine_body, [((ROWS, DV), F32)], [VM] * 3, [*hidden, kept_far], "far_mine", flops=2 * ROWS * DV * DV, moved=2 * DV * DV
    )
    for half in range(2):
        far += call(
            functools.partial(far_body, half), [((HALF, DV), BF)], [VM] * 3, [mine, other[half], theirs_far], f"far{half}",
            flops=2 * HALF * DV * DV, moved=2 * DV * DV, after=far,
        )
    via3, via1 = y_flip(far[0], 3), y_flip(far[1], 1)
    top1, low1, top3, low3 = partial(hidden, other, kept, theirs, (F32, BF, BF, F32), "beside", after=far)
    from1_low, from3_top = y_flip(low1, 1), y_flip(top3, 3)
    from1_top, from3_low = y_flip(added(top1, via3), 1), y_flip(added(low3, via1), 3)
    own = call(
        own_body, [((HALF, DV), F32)] * 2, [VM] * 8, [*hidden, *other, kept, theirs, from3_top, from1_low], "own",
        flops=4 * ROWS * DV * DV, moved=8 * DV * DV,
    )
    (out,) = call(
        final_body, [((ROWS, DV), BF)], [VM] * 4, [*own, from1_top, from3_low], "final", moved=ROWS * DV * 2,
    )
    return out


def solution(mesh):
    in_specs = (P("ctx", "tp"),) + (P(None, "tp"),) * 4 + (P("tp", None), P("tp", "ctx"))
    return jax.shard_map(
        shards, mesh=mesh, in_specs=in_specs, out_specs=P("ctx", "tp"), check_vma=False
    )
```
